256 devices in a mesh: row: 16 (over y_lo, x, core), col: 16 (over y_hi, z).
Axes of the slice: x: 4, y: 4 (y_hi: 2, y_lo: 2; y = y_hi * 2 + y_lo), z: 8, core: 2. Of those that a mesh axis runs over, the one named last changes fastest.
Arguments:
- frame_first: float32 [4, 4096, 4096], P(None, 'row', 'col'), may hold values from -10 to 10
- frame_second: float32 [4, 4096, 4096], P(None, 'row', 'col'), may hold values from -10 to 10
- shifts: int32 [16, 16, 2], P('row', 'col'), may hold values from -4 to 4, as said below
Outputs:
- flow_field: float32 [2, 4096, 4096], P(None, 'row', 'col')
- coarse_flow: float32 [2, 512, 512], P(None, 'row', 'col')
The draws below stay inside these ranges and needn't reach their ends.
Inputs may be any that keep to these rules, and one draw needn't show every extreme that they name: `shifts`: some tile has displacement 4 along rows and some tile -4 along columns.
All inputs are finite; a program needn't handle non-finite values.
Results may differ from the reference program's by a relative error of at most 0.0003.
Values sent between devices are 32-bit elements; how exact they have to be, the bound alone decides.
A program may use at most 64 MiB of HBM per device.

```python
import math
import jax
import jax.numpy as jnp
from jax import lax

BANDS = 4
TH = 256
TW = 256
FACTOR = 8
MAXD = 4
ITERS_C = 3
ITERS_F = 3
TILES_R = 16
TILES_C = 16
NX = 4096
NY = 4096
CNX = 512
CNY = 512


def wave_pattern(key, shift_rows, shift_cols):
    periods = jax.random.uniform(jax.random.fold_in(key, 11), (BANDS, 3, 2), jnp.float32, 24.0, 160.0)
    phases = jax.random.uniform(jax.random.fold_in(key, 12), (BANDS, 3, 2), jnp.float32, 0.0, 2.0 * math.pi)
    amplitudes = jax.random.uniform(jax.random.fold_in(key, 13), (BANDS, 3), jnp.float32, 0.5, 1.5)
    row_coords = jnp.arange(NX, dtype=jnp.float32)[None, :, None] + shift_rows
    col_coords = jnp.arange(NY, dtype=jnp.float32)[None, None, :] + shift_cols
    pattern = jnp.zeros((BANDS, NX, NY), jnp.float32)
    for term_index in range(3):
        along_rows = jnp.sin(2.0 * math.pi * row_coords / periods[:, term_index, 0][:, None, None] + phases[:, term_index, 0][:, None, None])
        along_cols = jnp.cos(2.0 * math.pi * col_coords / periods[:, term_index, 1][:, None, None] + phases[:, term_index, 1][:, None, None])
        pattern = pattern + amplitudes[:, term_index][:, None, None] * along_rows * along_cols
    return pattern


def noise_field(key):
    return 0.7 * jax.random.truncated_normal(key, -4.0, 4.0, (BANDS, NX, NY), jnp.float32)


def draw_frame_first(key, part):
    return wave_pattern(key, 0.0, 0.0) + noise_field(jax.random.fold_in(key, 1))


def draw_frame_second(key, part):
    return wave_pattern(key, 1.5, -2.5) + noise_field(jax.random.fold_in(key, 2))


def draw_shifts(key, part):
    values = jax.random.randint(jax.random.fold_in(key, 21), (TILES_R, TILES_C, 2), -MAXD, MAXD + 1, dtype=jnp.int32)
    return values.at[0, 0, 0].set(MAXD).at[0, 0, 1].set(-MAXD)


def setup_inputs(seed: int = 0) -> dict:
    streams_of = jax.random.split(jax.random.key(seed), 4)
    frame_first = draw_frame_first(jax.random.fold_in(streams_of[3], 71), 0)
    frame_second = draw_frame_second(jax.random.fold_in(streams_of[3], 71), 0)
    shifts = draw_shifts(jax.random.fold_in(streams_of[3], 71), 0)
    return {"frame_first": frame_first, "frame_second": frame_second, "shifts": shifts}


tau_step = 0.25
sigma_step = 0.25
data_weight = 0.3
smooth_weight = 0.3

def diff_rows(field_in):
    padded = jnp.pad(field_in, ((0, 0), (1, 1), (0, 0)))
    return 0.5 * (padded[:, 2:, :] - padded[:, :-2, :])

def diff_cols(field_in):
    padded = jnp.pad(field_in, ((0, 0), (0, 0), (1, 1)))
    return 0.5 * (padded[:, :, 2:] - padded[:, :, :-2])

def primal_dual(initial, grad_rows, grad_cols, offset, iterations):
    flow_now = initial
    extrapolated = initial
    dual_rows = jnp.zeros_like(initial)
    dual_cols = jnp.zeros_like(initial)
    dual_data = jnp.zeros_like(offset)
    for iteration in range(iterations):
        dual_rows = dual_rows + sigma_step * diff_rows(extrapolated)
        dual_cols = dual_cols + sigma_step * diff_cols(extrapolated)
        shrink_factor = jnp.maximum(1.0, jnp.sqrt(dual_rows * dual_rows + dual_cols * dual_cols) / smooth_weight)
        dual_rows = dual_rows / shrink_factor
        dual_cols = dual_cols / shrink_factor
        residual = offset + grad_rows * extrapolated[0:1] + grad_cols * extrapolated[1:2]
        dual_data = jnp.clip(dual_data + sigma_step * residual, -data_weight, data_weight)
        divergence = diff_rows(dual_rows) + diff_cols(dual_cols)
        data_pull = jnp.stack([lax.optimization_barrier(jnp.sum(dual_data * grad_rows, axis=0)), lax.optimization_barrier(jnp.sum(dual_data * grad_cols, axis=0))])
        flow_next = flow_now + tau_step * (divergence - data_pull)
        extrapolated = 2.0 * flow_next - flow_now
        flow_now = flow_next
    return flow_now

def reference(frame_first, frame_second, shifts):
    band_count = frame_first.shape[0]
    coarse_first = frame_first.reshape(band_count, CNX, FACTOR, CNY, FACTOR).mean(axis=(2, 4))
    coarse_second = frame_second.reshape(band_count, CNX, FACTOR, CNY, FACTOR).mean(axis=(2, 4))
    coarse_result = primal_dual(jnp.zeros((2, CNX, CNY), jnp.float32), diff_rows(coarse_second), diff_cols(coarse_second), coarse_second - coarse_first, ITERS_C)
    initial = FACTOR * jnp.repeat(jnp.repeat(coarse_result, FACTOR, axis=1), FACTOR, axis=2)
    rim_width = MAXD + 1
    padded = jnp.pad(frame_second, ((0, 0), (rim_width, rim_width), (rim_width, rim_width)))
    row_ids = jnp.arange(TILES_R, dtype=jnp.int32)
    col_ids = jnp.arange(TILES_C, dtype=jnp.int32)

    def tile_window(tile_row, tile_col):
        offsets = shifts[tile_row, tile_col]
        corner = (jnp.int32(0), (tile_row * TH + MAXD + offsets[0]).astype(jnp.int32), (tile_col * TW + MAXD + offsets[1]).astype(jnp.int32))
        return lax.dynamic_slice(padded, corner, (band_count, TH + 2, TW + 2))

    def window_row(tile_row):

        def window_one(tile_col):
            return tile_window(tile_row, tile_col)
        return jax.vmap(window_one)(col_ids)
    windows = jax.vmap(window_row)(row_ids)

    def assemble(blocks):
        return blocks.transpose(2, 0, 3, 1, 4).reshape(band_count, NX, NY)
    warped = assemble(windows[:, :, :, 1:-1, 1:-1])
    grad_rows = assemble(0.5 * (windows[:, :, :, 2:, 1:-1] - windows[:, :, :, :-2, 1:-1]))
    grad_cols = assemble(0.5 * (windows[:, :, :, 1:-1, 2:] - windows[:, :, :, 1:-1, :-2]))
    offset = warped - frame_first - grad_rows * initial[0:1] - grad_cols * initial[1:2]
    flow_result = primal_dual(initial, grad_rows, grad_cols, offset, ITERS_F)
    return (flow_result, coarse_result)
```

```python
import jax
import jax.numpy as jnp
from jax import lax
from jax.experimental import pallas as pl
from jax.experimental.pallas import tpu as pltpu
from jax.sharding import PartitionSpec as P

FACTOR = 8
TAU = 0.25
SIGMA = 0.25
LAM = 0.3
ALPHA = 0.3
BANDS = 4
T = 256
CT = T // FACTOR
OFF = 16
ROWS = T + 2 * OFF
PANELS = 3
WIDE = 128 * PANELS
CROWS = CT + 16
F32 = jnp.float32
BF16 = jnp.bfloat16
DIRECTIONS = [(-1, -1), (-1, 0), (-1, 1), (0, -1), (0, 1), (1, -1), (1, 0), (1, 1)]


def split3(x):
    hi = x.astype(BF16)
    rest = x - hi.astype(F32)
    mid = rest.astype(BF16)
    low = (rest - mid.astype(F32)).astype(BF16)
    return hi, mid, low


def dot_split(x, w, parts):
    total = None
    for piece in split3(x)[:parts]:
        term = jnp.dot(piece, w, preferred_element_type=F32)
        total = term if total is None else total + term
    return total


def roll(x, amount, axis):
    amount = amount % x.shape[axis]
    return x if amount == 0 else pltpu.roll(x, amount, axis)


def next_minus_prev(x, axis):
    return roll(x, -1, axis) - roll(x, 1, axis)


def following(x):
    return jnp.concatenate([x[1:], x[:1]], axis=0)


def preceding(x):
    return jnp.concatenate([x[-1:], x[:-1]], axis=0)


def across(x):
    lane = lax.broadcasted_iota(jnp.int32, x.shape, 2)
    ahead, behind = roll(x, -1, 2), roll(x, 1, 2)
    return jnp.where(lane == 127, following(ahead), ahead) - jnp.where(lane == 0, preceding(behind), behind)


def shrink(pr, pc):
    return jnp.minimum(1.0, ALPHA * lax.rsqrt(pr * pr + pc * pc))


def kernel(
    f1_ref, f2_ref, sh_ref, flow_ref, coarse_ref,
    s2, f1v, g, q, u, ub, prv, pcv, ti, ce,
    p1, e1, h1, k1, p2, e2, h2, k2,
    local_sem, send_sem, recv_sem,
):
    me_r, me_c = lax.axis_index("row"), lax.axis_index("col")
    n_r, n_c = lax.axis_size("row"), lax.axis_size("col")

    def device(direction):
        dr, dc = direction
        return (lax.rem(me_r + dr + n_r, n_r), lax.rem(me_c + dc + n_c, n_c))

    barrier = pltpu.get_barrier_semaphore()
    for direction in DIRECTIONS:
        pl.semaphore_signal(barrier, inc=1, device_id=device(direction), device_id_type=pl.DeviceIdType.MESH)
    gets = []
    for ref, kept in ((f2_ref, lambda k: s2.at[:, k, pl.ds(OFF, T), :]), (f1_ref, lambda k: f1v.at[:, k])):
        for k in range(2):
            copy = pltpu.make_async_copy(ref.at[:, :, pl.ds(128 * k, 128)], kept(k), local_sem.at[len(gets)])
            copy.start()
            gets.append(copy)

    sends = []

    def send(src, dst, direction):
        slot = len(sends)
        copy = pltpu.make_async_remote_copy(
            src_ref=src, dst_ref=dst, send_sem=send_sem.at[slot], recv_sem=recv_sem.at[slot],
            device_id=device(direction), device_id_type=pl.DeviceIdType.MESH,
        )
        copy.start()
        sends.append(copy)
        return copy

    lane = lax.broadcasted_iota(jnp.int32, (8, 128), 1)
    tall = lax.broadcasted_iota(jnp.int32, (128, 128), 1)
    gets[0].wait()
    gets[1].wait()

    def pack1(i, carry):
        rows = pl.ds(pl.multiple_of(OFF + 8 * i, 8), 8)
        acc = jnp.zeros((8, 128), F32)
        for b in range(BANDS):
            edge = jnp.where(lane < 8, s2[b, 0, rows, :], s2[b, 1, rows, :])
            acc = jnp.where(lane // 16 == b, roll(edge, 16 * b + 8, 1), acc)
        p1[pl.ds(pl.multiple_of(8 * i, 8), 8), :] = acc
        return carry

    lax.fori_loop(0, T // 8, pack1, 0, unroll=4)
    low = p1[0:128, :]
    high = p1[128:256, :]
    odd8 = (tall // 8) % 2 == 1
    e1[0] = jnp.where(odd8, high, roll(low, -8, 1))
    e1[1] = jnp.where(odd8, roll(high, 8, 1), low)
    gets[2].wait()
    gets[3].wait()

    col_id = lax.broadcasted_iota(jnp.int32, (128, 128), 0) // FACTOR
    lane_id = lax.broadcasted_iota(jnp.int32, (128, 128), 1)
    row_sum = (
        lax.broadcasted_iota(jnp.int32, (CT, T), 1) // FACTOR == lax.broadcasted_iota(jnp.int32, (CT, T), 0)
    ).astype(F32).astype(BF16)
    for frame in range(2):
        total = jnp.zeros((T, 128), F32)
        for b in range(BANDS):
            for k in range(2):
                block = f1v[b, k] if frame == 0 else s2[b, k, OFF:OFF + T, :]
                weights = jnp.where(lane_id - CT * b - 16 * k == col_id, 1.0 / 64.0, 0.0).astype(BF16)
                total = total + dot_split(block, weights, 2)
        hi, mid, _ = split3(total)
        ce[1, frame, 8:8 + CT, :] = (
            jnp.dot(row_sum, hi, preferred_element_type=F32) + jnp.dot(row_sum, mid, preferred_element_type=F32)
        )

    pl.semaphore_wait(barrier, len(DIRECTIONS))

    round1 = []
    for direction in DIRECTIONS:
        dr, dc = direction
        src_row = {-1: 8, 0: 8, 1: CT}[dr]
        dst_row = {-1: 8 + CT, 0: 8, 1: 0}[dr]
        count = CT if dr == 0 else 8
        round1.append(send(
            ce.at[1, :, pl.ds(src_row, count), :], ce.at[1 - dc, :, pl.ds(dst_row, count), :], direction
        ) if dc != 0 else send(
            ce.at[1, :, pl.ds(src_row, count), :], ce.at[1, :, pl.ds(dst_row, count), :], direction
        ))
    top, bottom = pl.ds(0, 8), pl.ds(T - 8, 8)
    round1.append(send(s2.at[:, pl.ds(0, 2), pl.ds(OFF, 8)], s2.at[:, pl.ds(0, 2), pl.ds(OFF + T, 8)], (-1, 0)))
    round1.append(send(s2.at[:, pl.ds(0, 2), pl.ds(OFF + T - 8, 8)], s2.at[:, pl.ds(0, 2), pl.ds(OFF - 8, 8)], (1, 0)))
    round1.append(send(e1.at[0], h1.at[0], (0, -1)))
    round1.append(send(e1.at[1], h1.at[1], (0, 1)))
    for dr in (-1, 1):
        for dc in (-1, 1):
            round1.append(send(
                p1.at[top if dr == -1 else bottom, :],
                k1.at[1 if dr == -1 else 0, 1 if dc == -1 else 0], (dr, dc),
            ))
    for copy in round1:
        copy.wait()

    keep_lane = jnp.where(lane[0:1] < 64, jnp.where(me_c == n_c - 1, 0.0, 1.0), jnp.where(me_c == 0, 0.0, 1.0))
    from_right, from_left = h1[0], roll(h1[1], -8, 1)
    for half in range(2):
        mix = jnp.where((tall // 8) % 2 == half, from_right, from_left)
        for b in range(BANDS):
            s2[b, 2, OFF + 128 * half:OFF + 128 * half + 128, :] = roll(mix, -(16 * b + 8 * half), 1) * keep_lane
    for side in range(2):
        mix = jnp.where((lane // 8) % 2 == 0, k1[side, 0], k1[side, 1])
        base = OFF - 8 if side == 0 else OFF + T
        for b in range(BANDS):
            s2[b, 2, base:base + 8, :] = roll(mix, -(16 * b + 8), 1) * keep_lane

    @pl.when(me_r == 0)
    def _():
        s2[:, :, OFF - 8:OFF, :] = jnp.zeros((BANDS, PANELS, 8, 128), F32)

    @pl.when(me_r == n_r - 1)
    def _():
        s2[:, :, OFF + T:OFF + T + 8, :] = jnp.zeros((BANDS, PANELS, 8, 128), F32)

    shift_r, shift_c = sh_ref[0, 0, 0], sh_ref[0, 0, 1]
    amount = jnp.where(shift_c > 0, 128 - shift_c, -shift_c)
    panel_lane = lax.broadcasted_iota(jnp.int32, (PANELS, 8, 128), 2)
    over = panel_lane + shift_c >= 128
    under = panel_lane + shift_c < 0

    def shifted(x):
        turned = pltpu.roll(x, amount, 2)
        return jnp.where(over, following(turned), jnp.where(under, preceding(turned), turned))

    def window(s, carry):
        rows = pl.ds(pl.multiple_of(OFF + 8 * s, 8), 8)
        start = OFF + 8 * s + shift_r
        packed = jnp.zeros((8, 128), F32)
        for b in range(BANDS):
            here = shifted(s2[b, :, pl.ds(start, 8), :])
            down = shifted(s2[b, :, pl.ds(start + 1, 8), :] - s2[b, :, pl.ds(start - 1, 8), :])
            fields = (
                0.5 * down[:2],
                0.5 * across(here)[:2],
                here[:2] - f1v[b, :, pl.ds(pl.multiple_of(8 * s, 8), 8), :],
            )
            for kind in range(3):
                f = BANDS * kind + b
                g[f, 0:2, rows, :] = fields[kind]
                edge = jnp.where(lane < 4, fields[kind][0], fields[kind][1])
                packed = jnp.where(lane // 8 == f, roll(edge, 8 * f + 4, 1), packed)
        p2[pl.ds(pl.multiple_of(8 * s, 8), 8), :] = packed
        return carry

    lax.fori_loop(0, T // 8, window, 0)
    low = p2[0:128, :]
    high = p2[128:256, :]
    odd4 = (tall // 4) % 2 == 1
    e2[0] = jnp.where(odd4, high, roll(low, -4, 1))
    e2[1] = jnp.where(odd4, roll(high, 4, 1), low)

    round2 = [
        send(e2.at[0], h2.at[0], (0, -1)),
        send(e2.at[1], h2.at[1], (0, 1)),
        send(g.at[:, pl.ds(0, 2), pl.ds(OFF, 8)], g.at[:, pl.ds(0, 2), pl.ds(OFF + T, 8)], (-1, 0)),
        send(g.at[:, pl.ds(0, 2), pl.ds(OFF + T - 8, 8)], g.at[:, pl.ds(0, 2), pl.ds(OFF - 8, 8)], (1, 0)),
    ]
    for dr in (-1, 1):
        for dc in (-1, 1):
            round2.append(send(
                p2.at[top if dr == -1 else bottom, :],
                k2.at[1 if dr == -1 else 0, 1 if dc == -1 else 0], (dr, dc),
            ))

    crow = lax.broadcasted_iota(jnp.int32, (CROWS, 128), 0) - 8 + me_r * CT
    clane = lax.broadcasted_iota(jnp.int32, (CROWS, 128), 1)
    ccol = jnp.where(clane < 64, clane, clane - 128) + me_c * CT
    inside = (crow >= 0) & (crow < n_r * CT) & (ccol >= 0) & (ccol < n_c * CT)
    mask = jnp.where(inside, 1.0, 0.0)
    means = []
    for frame in range(2):
        mine, right, left = ce[1, frame], roll(ce[2, frame], CT, 1), roll(ce[0, frame], -CT, 1)
        bands = []
        for b in range(BANDS):
            mix = jnp.where(clane // CT == (b + 1) % 4, right, jnp.where(clane // CT == (b + 3) % 4, left, mine))
            bands.append(roll(mix, -CT * b, 1) * mask)
        means.append(bands)
    grad_r = [0.5 * next_minus_prev(x, 0) for x in means[1]]
    grad_c = [0.5 * next_minus_prev(x, 1) for x in means[1]]
    off = [means[1][b] - means[0][b] for b in range(BANDS)]
    now = [jnp.zeros((CROWS, 128), F32)] * 2
    bar = now
    dual_r, dual_c = list(now), list(now)
    data = [jnp.zeros((CROWS, 128), F32)] * BANDS
    for it in range(3):
        div = [0.0, 0.0]
        if it > 0:
            for c in range(2):
                pr = dual_r[c] + (0.5 * SIGMA) * next_minus_prev(bar[c], 0)
                pc = dual_c[c] + (0.5 * SIGMA) * next_minus_prev(bar[c], 1)
                k = shrink(pr, pc) * mask
                dual_r[c], dual_c[c] = pr * k, pc * k
                div[c] = 0.5 * (next_minus_prev(dual_r[c], 0) + next_minus_prev(dual_c[c], 1))
        pull = [0.0, 0.0]
        for b in range(BANDS):
            rho = off[b]
            if it > 0:
                rho = rho + grad_r[b] * bar[0] + grad_c[b] * bar[1]
            data[b] = jnp.clip(data[b] + SIGMA * rho, -LAM, LAM)
            pull = [pull[0] + data[b] * grad_r[b], pull[1] + data[b] * grad_c[b]]
        later = [(now[c] + TAU * (div[c] - pull[c])) * mask for c in range(2)]
        bar = [2.0 * later[c] - now[c] for c in range(2)]
        now = later
    for c in range(2):
        coarse_ref[c] = now[c][8:8 + CT, 0:CT]

    wide = lax.broadcasted_iota(jnp.int32, (128, WIDE), 1)
    source = jnp.where(wide < T + 64, wide // FACTOR, 128 - (WIDE - wide + FACTOR - 1) // FACTOR)
    spread = jnp.where(lax.broadcasted_iota(jnp.int32, (128, WIDE), 0) == source, float(FACTOR), 0.0).astype(BF16)
    for c in range(2):
        repeated = dot_split(now[c], spread, 3)
        for k in range(PANELS):
            ti[c, k] = repeated[:, 128 * k:128 * k + 128]

    def start_value(c, s):
        return jnp.broadcast_to(ti[c, :, pl.ds(s + 6, 1), :], (PANELS, 8, 128))

    def fill(s, carry):
        rows = pl.ds(pl.multiple_of(8 * s, 8), 8)
        for c in range(2):
            value = start_value(c, s)
            u[c, :, rows, :] = value
            ub[c, :, rows, :] = value
        return carry

    lax.fori_loop(1, ROWS // 8 - 1, fill, 0)

    for copy in round2:
        copy.wait()
    from_right, from_left = h2[0], roll(h2[1], -4, 1)
    for half in range(2):
        mix = jnp.where((tall // 4) % 2 == half, from_right, from_left)
        for f in range(3 * BANDS):
            g[f, 2, OFF + 128 * half:OFF + 128 * half + 128, :] = roll(mix, -(8 * f + 4 * half), 1)
    for side in range(2):
        mix = jnp.where((lane // 4) % 2 == 0, k2[side, 0], k2[side, 1])
        base = OFF - 8 if side == 0 else OFF + T
        for f in range(3 * BANDS):
            g[f, 2, base:base + 8, :] = roll(mix, -(8 * f + 4), 1)

    flane = panel_lane + 128 * lax.broadcasted_iota(jnp.int32, (PANELS, 8, 128), 0)
    fcol = jnp.where(flane < T + 64, flane, flane - WIDE) + me_c * T
    col_mask = jnp.where((fcol >= 0) & (fcol < n_c * T), 1.0, 0.0)

    def strip_mask(s):
        row = 8 * s - OFF + me_r * T
        return col_mask * jnp.where((row >= 0) & (row < n_r * T), 1.0, 0.0)

    for it in range(3):
        def dual(s, carry):
            base = 8 * s
            rows = pl.ds(pl.multiple_of(base, 8), 8)
            m = strip_mask(s)
            for c in range(2):
                pr = (0.5 * SIGMA) * (ub[c, :, pl.ds(base + 1, 8), :] - ub[c, :, pl.ds(base - 1, 8), :])
                pc = (0.5 * SIGMA) * across(ub[c, :, rows, :])
                if it > 0:
                    pr = prv[c, :, rows, :] + pr
                    pc = pcv[c, :, rows, :] + pc
                k = shrink(pr, pc) * m
                prv[c, :, rows, :] = pr * k
                pcv[c, :, rows, :] = pc * k
            return carry

        lax.fori_loop(1, ROWS // 8 - 1, dual, 0)

        def primal(s, carry):
            base = 8 * s
            rows = pl.ds(pl.multiple_of(base, 8), 8)
            m = strip_mask(s)
            if it > 0:
                step = [ub[c, :, rows, :] - start_value(c, s) for c in range(2)]
            pull = [0.0, 0.0]
            for b in range(BANDS):
                gr, gc, rho = g[b, :, rows, :], g[BANDS + b, :, rows, :], g[2 * BANDS + b, :, rows, :]
                if it > 0:
                    rho = q[b, :, rows, :] + SIGMA * (rho + gr * step[0] + gc * step[1])
                else:
                    rho = SIGMA * rho
                dq = jnp.clip(rho, -LAM, LAM)
                if it < 2:
                    q[b, :, rows, :] = dq
                pull = [pull[0] + dq * gr, pull[1] + dq * gc]
            for c in range(2):
                div = 0.5 * (
                    prv[c, :, pl.ds(base + 1, 8), :] - prv[c, :, pl.ds(base - 1, 8), :]
                    + across(pcv[c, :, rows, :])
                )
                was = u[c, :, rows, :]
                later = (was + TAU * (div - pull[c])) * m
                if it < 2:
                    u[c, :, rows, :] = later
                    ub[c, :, rows, :] = 2.0 * later - was
                else:
                    out_rows = pl.ds(pl.multiple_of(base - OFF, 8), 8)
                    for k in range(2):
                        flow_ref[c, out_rows, 128 * k:128 * k + 128] = later[k]
            return carry

        if it < 2:
            lax.fori_loop(1, ROWS // 8 - 1, primal, 0)
        else:
            lax.fori_loop(OFF // 8, (OFF + T) // 8, primal, 0)


def local(frame_first, frame_second, shifts):
    vmem = pltpu.VMEM
    return pl.pallas_call(
        kernel,
        out_shape=(
            jax.ShapeDtypeStruct((2, T, T), F32),
            jax.ShapeDtypeStruct((2, CT, CT), F32),
        ),
        in_specs=[
            pl.BlockSpec(memory_space=pl.ANY),
            pl.BlockSpec(memory_space=pl.ANY),
            pl.BlockSpec(memory_space=pltpu.SMEM),
        ],
        out_specs=(pl.BlockSpec(memory_space=vmem), pl.BlockSpec(memory_space=vmem)),
        scratch_shapes=[
            vmem((BANDS, PANELS, ROWS, 128), F32),
            vmem((BANDS, 2, T, 128), F32),
            vmem((3 * BANDS, PANELS, ROWS, 128), F32),
            vmem((BANDS, PANELS, ROWS, 128), F32),
            vmem((2, PANELS, ROWS, 128), F32),
            vmem((2, PANELS, ROWS, 128), F32),
            vmem((2, PANELS, ROWS, 128), F32),
            vmem((2, PANELS, ROWS, 128), F32),
            vmem((2, PANELS, CROWS, 128), F32),
            vmem((3, 2, CROWS, 128), F32),
            vmem((T, 128), F32), vmem((2, 128, 128), F32), vmem((2, 128, 128), F32), vmem((2, 2, 8, 128), F32),
            vmem((T, 128), F32), vmem((2, 128, 128), F32), vmem((2, 128, 128), F32), vmem((2, 2, 8, 128), F32),
            pltpu.SemaphoreType.DMA((4,)),
            pltpu.SemaphoreType.DMA((24,)),
            pltpu.SemaphoreType.DMA((24,)),
        ],
        compiler_params=pltpu.CompilerParams(
            collective_id=0, has_side_effects=True, vmem_limit_bytes=48 * 1024 * 1024
        ),
    )(frame_first, frame_second, shifts)


def solution(mesh):
    return jax.shard_map(
        local,
        mesh=mesh,
        in_specs=(P(None, "row", "col"), P(None, "row", "col"), P("row", "col", None)),
        out_specs=(P(None, "row", "col"), P(None, "row", "col")),
        check_vma=False,
    )
```

```python
import jax
import jax.numpy as jnp
from jax import lax
from jax.experimental import pallas as pl
from jax.experimental.pallas import tpu as pltpu
from jax.sharding import PartitionSpec as P

FACTOR = 8
TAU = 0.25
SIGMA = 0.25
LAM = 0.3
ALPHA = 0.3
BANDS = 4
T = 256
CT = T // FACTOR
OFF = 24
ROWS = T + 2 * OFF
FIRST = OFF - 8
STRIPS = T // 8 + 2
UNROLL = STRIPS // 2
PANELS = 3
DEEP = 9
THIN = 4
CROWS = CT + 16
F32 = jnp.float32
BF16 = jnp.bfloat16
DIRECTIONS = [(-1, -1), (-1, 1), (1, -1), (1, 1), (0, -1), (0, 1), (-1, 0), (1, 0)]


def split3(x):
    hi = x.astype(BF16)
    rest = x - hi.astype(F32)
    mid = rest.astype(BF16)
    low = (rest - mid.astype(F32)).astype(BF16)
    return hi, mid, low


def dot_split(x, w, parts):
    total = None
    for piece in split3(x)[:parts]:
        term = jnp.dot(piece, w, preferred_element_type=F32)
        total = term if total is None else total + term
    return total


def roll(x, amount, axis):
    amount = amount % x.shape[axis]
    return x if amount == 0 else pltpu.roll(x, amount, axis)


def next_minus_prev(x, axis):
    return roll(x, -1, axis) - roll(x, 1, axis)


def following(x):
    return jnp.concatenate([x[1:], x[:1]], axis=0)


def preceding(x):
    return jnp.concatenate([x[-1:], x[:-1]], axis=0)


def across(x):
    lane = lax.broadcasted_iota(jnp.int32, x.shape, 2)
    ahead, behind = roll(x, -1, 2), roll(x, 1, 2)
    return jnp.where(lane == 127, following(ahead), ahead) - jnp.where(lane == 0, preceding(behind), behind)


def shrink(square):
    return jnp.minimum(1.0, ALPHA * lax.rsqrt(square))


def aligned(start, size=8):
    return pl.ds(pl.multiple_of(start, 8), size)


def kernel(
    f1_ref, f2_ref, sh_ref, flow_ref, coarse_ref,
    s2, f1v, g, a, p1, u, ub, prv, pcv, tc, ce, cs, cr,
    pack, es, er, kr, eq, own, shs, shr,
    local_sem, send_sem, recv_sem,
):
    me_r, me_c = lax.axis_index("row"), lax.axis_index("col")
    n_r, n_c = lax.axis_size("row"), lax.axis_size("col")

    def device(direction):
        dr, dc = direction
        return (lax.rem(me_r + dr + n_r, n_r), lax.rem(me_c + dc + n_c, n_c))

    barrier = pltpu.get_barrier_semaphore()
    for direction in DIRECTIONS:
        pl.semaphore_signal(barrier, inc=1, device_id=device(direction), device_id_type=pl.DeviceIdType.MESH)
    gets = []
    for ref, kept in ((f2_ref, s2), (f1_ref, f1v)):
        for k in range(2):
            copy = pltpu.make_async_copy(
                ref.at[:, :, pl.ds(128 * k, 128)], kept.at[:, k, pl.ds(OFF, T), :], local_sem.at[len(gets)]
            )
            copy.start()
            gets.append(copy)
    my_shift = (sh_ref[0, 0, 0], sh_ref[0, 0, 1])
    sub8 = lax.broadcasted_iota(jnp.int32, (8, 128), 0)
    shs[...] = jnp.where(sub8 == 0, my_shift[0], my_shift[1])

    sends = []

    def send(src, dst, direction):
        slot = len(sends)
        copy = pltpu.make_async_remote_copy(
            src_ref=src, dst_ref=dst, send_sem=send_sem.at[slot], recv_sem=recv_sem.at[slot],
            device_id=device(direction), device_id_type=pl.DeviceIdType.MESH,
        )
        copy.start()
        sends.append(copy)

    lane = lax.broadcasted_iota(jnp.int32, (8, 128), 1)
    place = lane % 16
    right_side = lane < 64
    tall = lax.broadcasted_iota(jnp.int32, (T // 2, 128), 1) < 64
    for copy in gets:
        copy.wait()

    def packing(i, carry):
        rows = aligned(OFF + 8 * i)
        acc = jnp.zeros((8, 128), F32)
        for b in range(BANDS):
            left2, right2, left1, right1 = s2[b, 0, rows, :], s2[b, 1, rows, :], f1v[b, 0, rows, :], f1v[b, 1, rows, :]
            left = jnp.where(place < 6, roll(left1, 16 * b, 1), roll(left2, 16 * b + 6, 1))
            right = jnp.where(place < 10, roll(right2, 16 * b + 74, 1), roll(right1, 16 * b + 78, 1))
            acc = jnp.where(lane // 16 == b, left, jnp.where(lane // 16 == b + 4, right, acc))
        pack[aligned(8 * i), :] = acc
        return carry

    lax.fori_loop(0, T // 8, packing, 0, unroll=8)
    upper, lower = pack[0:128, :], pack[128:256, :]
    es[0] = jnp.where(tall, upper, roll(lower, 64, 1))
    es[1] = jnp.where(tall, roll(upper, 64, 1), lower)

    col_id = lax.broadcasted_iota(jnp.int32, (128, 128), 0) // FACTOR
    lane_id = lax.broadcasted_iota(jnp.int32, (128, 128), 1)
    row_sum = (
        lax.broadcasted_iota(jnp.int32, (CT, T), 1) // FACTOR == lax.broadcasted_iota(jnp.int32, (CT, T), 0)
    ).astype(F32).astype(BF16)
    for frame in range(2):
        total = jnp.zeros((T, 128), F32)
        for b in range(BANDS):
            for k in range(2):
                block = (f1v if frame == 0 else s2)[b, k, OFF:OFF + T, :]
                weights = jnp.where(lane_id - CT * b - 16 * k == col_id, 1.0 / 64.0, 0.0).astype(BF16)
                total = total + dot_split(block, weights, 2)
        hi, mid, _ = split3(total)
        ce[frame, 8:8 + CT, :] = (
            jnp.dot(row_sum, hi, preferred_element_type=F32) + jnp.dot(row_sum, mid, preferred_element_type=F32)
        )
    group = (lax.broadcasted_iota(jnp.int32, (16, 128), 1) % CT) // 8
    edge_l = edge_r = jnp.zeros((16, 128), F32)
    for frame in range(2):
        for half in range(2):
            n = 2 * frame + half
            piece = ce[frame, 8 + 16 * half:24 + 16 * half, :]
            edge_l = jnp.where(group == n, roll(piece, 8 * n, 1), edge_l)
            edge_r = jnp.where(group == n, roll(piece, 8 * n - 24, 1), edge_r)
    cs[0] = edge_l
    cs[1] = edge_r

    pl.semaphore_wait(barrier, len(DIRECTIONS))

    def send_rows(dr, dc, seen):
        for frame in range(2):
            send(
                ce.at[frame, pl.ds(8 if dr < 0 else CT, 8), :], cr.at[seen, pl.ds(8 * frame, 8), :], (dr, dc)
            )

    for dr, dc in DIRECTIONS:
        seen = DIRECTIONS.index((-dr, -dc))
        if dr != 0 and dc != 0:
            send(pack.at[pl.ds(0 if dr < 0 else T - 16, 16), :], kr.at[seen], (dr, dc))
            send_rows(dr, dc, seen)
        elif dr == 0:
            side = 0 if dc < 0 else 1
            send(es.at[side], er.at[side], (dr, dc))
            send(cs.at[side], cr.at[seen], (dr, dc))
        else:
            send_rows(dr, dc, seen)
            from2, to2 = (OFF, OFF + T) if dr < 0 else (OFF + T - DEEP, OFF - DEEP)
            from1, to1 = (OFF, OFF + T) if dr < 0 else (OFF + T - THIN, OFF - THIN)
            both = pl.ds(0, 2)
            send(s2.at[:, both, pl.ds(from2, DEEP), :], s2.at[:, both, pl.ds(to2, DEEP), :], (dr, dc))
            send(f1v.at[:, both, pl.ds(from1, THIN), :], f1v.at[:, both, pl.ds(to1, THIN), :], (dr, dc))
        send(shs, shr.at[seen], (dr, dc))

    def own_edge(start):
        acc = jnp.zeros((8, 128), F32)
        for b in range(BANDS):
            left, right = s2[b, 0, aligned(start), :], s2[b, 1, aligned(start), :]
            acc = jnp.where(lane // 16 == b, roll(right, 16 * b + 6, 1), acc)
            acc = jnp.where(lane // 16 == b + 4, roll(left, 16 * b + 74, 1), acc)
        return acc

    def owning(i, carry):
        own[aligned(OFF + 8 * i), :] = own_edge(OFF + 8 * i)
        return carry

    lax.fori_loop(0, T // 8, owning, 0, unroll=8)

    for copy in sends:
        copy.wait()

    def at(direction):
        return DIRECTIONS.index(direction)

    shift_at = {d: (shr[at(d), 0, 0], shr[at(d), 1, 0]) for d in DIRECTIONS}

    keep_lane = jnp.where(
        lane[0:1] < 64, jnp.where(me_c == n_c - 1, 0.0, 1.0), jnp.where(me_c == 0, 0.0, 1.0)
    )
    eq[OFF:OFF + 128, :] = jnp.where(tall, er[0], roll(er[1], 64, 1)) * keep_lane
    eq[OFF + 128:OFF + 256, :] = jnp.where(tall, roll(er[0], 64, 1), er[1]) * keep_lane
    side16 = lax.broadcasted_iota(jnp.int32, (16, 128), 1) < 64
    eq[OFF - 16:OFF, :] = jnp.where(side16, kr[at((-1, 1))], kr[at((-1, -1))]) * keep_lane
    eq[OFF + T:OFF + T + 16, :] = jnp.where(side16, kr[at((1, 1))], kr[at((1, -1))]) * keep_lane

    @pl.when(me_r == 0)
    def _():
        s2[:, 0:2, OFF - 16:OFF, :] = jnp.zeros((BANDS, 2, 16, 128), F32)
        eq[OFF - 16:OFF, :] = jnp.zeros((16, 128), F32)

    @pl.when(me_r == n_r - 1)
    def _():
        s2[:, 0:2, OFF + T:OFF + T + 16, :] = jnp.zeros((BANDS, 2, 16, 128), F32)
        eq[OFF + T:OFF + T + 16, :] = jnp.zeros((16, 128), F32)

    for start in (OFF - 16, OFF - 8, OFF + T, OFF + T + 8):
        own[start:start + 8, :] = own_edge(start)

    theirs = (right_side & (place >= 6)) | ((lane >= 64) & (place < 10))

    def third(i, carry):
        rows = aligned(OFF - 16 + 8 * i)
        x = eq[rows, :]
        mix = jnp.where((place >= 6) & (place < 13), x, roll(x, 60, 1))
        for b in range(BANDS):
            s2[b, 2, rows, :] = roll(mix, -(16 * b + 6), 1)
        own[rows, :] = jnp.where(theirs, x, own[rows, :])
        return carry

    lax.fori_loop(0, STRIPS + 2, third, 0, unroll=9)

    panel_lane = lax.broadcasted_iota(jnp.int32, (PANELS, 8, 128), 2)

    def back(shift):
        return jnp.where(shift > 0, 128 - shift, -shift)

    def store_data(fields, b, panels, rows, pull):
        dr, dc, wf = fields
        first = jnp.clip(wf, -LAM, LAM)
        g[b, panels, rows, :] = dr
        g[BANDS + b, panels, rows, :] = dc
        g[2 * BANDS + b, panels, rows, :] = wf
        a[b, panels, rows, :] = first + wf
        return [pull[0] + first * dr, pull[1] + first * dc]

    def window(base, shift):
        rows = aligned(base)
        start = base + shift[0]
        amount = back(shift[1])
        over = panel_lane + shift[1] >= 128
        under = panel_lane + shift[1] < 0

        def shifted(x):
            turned = pltpu.roll(x, amount, 2)
            return jnp.where(over, following(turned), jnp.where(under, preceding(turned), turned))

        pull = [0.0, 0.0]
        for b in range(BANDS):
            here = shifted(s2[b, :, pl.ds(start, 8), :])
            down = shifted(s2[b, :, pl.ds(start + 1, 8), :] - s2[b, :, pl.ds(start - 1, 8), :])
            fields = (down[:2], across(here)[:2], SIGMA * (here[:2] - f1v[b, :, rows, :]))
            pull = store_data(fields, b, slice(0, 2), rows, pull)
        for c in range(2):
            p1[c, 0:2, rows, :] = pull[c]

    def window_loop(i, carry):
        window(OFF + 8 * i, my_shift)
        return carry

    lax.fori_loop(0, T // 8, window_loop, 0, unroll=4)
    window(OFF - 8, shift_at[(-1, 0)])
    window(OFF + T, shift_at[(1, 0)])

    def edge(base, right, left):
        rows = aligned(base)

        def pick(x, y):
            return jnp.where(right_side, pltpu.roll(x, back(right[1]), 1), pltpu.roll(y, back(left[1]), 1))

        def near(shift, step):
            return own[pl.ds(base + shift[0] + step, 8), :]

        here = pick(near(right, 0), near(left, 0))
        down = pick(near(right, 1) - near(right, -1), near(left, 1) - near(left, -1))
        x = eq[rows, :]
        first = jnp.where(right_side, roll(x, 6, 1), roll(x, -4, 1))
        kinds = []
        for field in (down, next_minus_prev(here, 1), SIGMA * (here - first)):
            kinds.append(jnp.where((place >= 6) & (place < 10), field, roll(field, 60, 1)))
        pull = [0.0, 0.0]
        for b in range(BANDS):
            fields = [roll(kind, -(16 * b + 6), 1) for kind in kinds]
            pull = store_data(fields, b, 2, rows, pull)
        for c in range(2):
            p1[c, 2, rows, :] = pull[c]

    def edge_loop(i, carry):
        edge(OFF + 8 * i, shift_at[(0, 1)], shift_at[(0, -1)])
        return carry

    lax.fori_loop(0, T // 8, edge_loop, 0, unroll=8)
    edge(OFF - 8, shift_at[(-1, 1)], shift_at[(-1, -1)])
    edge(OFF + T, shift_at[(1, 1)], shift_at[(1, -1)])

    crow = lax.broadcasted_iota(jnp.int32, (CROWS, 128), 0) - 8 + me_r * CT
    clane = lax.broadcasted_iota(jnp.int32, (CROWS, 128), 1)
    ccol = jnp.where(clane < 64, clane, clane - 128) + me_c * CT
    mask = jnp.where((crow >= 0) & (crow < n_r * CT) & (ccol >= 0) & (ccol < n_c * CT), 1.0, 0.0)
    means = []
    for frame in range(2):
        def column(dc):
            parts = [cr[at((-1, dc)), 8 * frame:8 * frame + 8, :]]
            turn = CT * dc
            if dc == 0:
                parts.append(ce[frame, 8:8 + CT, :])
            else:
                for half in range(2):
                    n = 2 * frame + half
                    parts.append(roll(cr[at((0, dc))], (0 if dc > 0 else 24) - 8 * n, 1))
            parts.append(cr[at((1, dc)), 8 * frame:8 * frame + 8, :])
            return roll(jnp.concatenate(parts, axis=0), turn, 1)

        mine, right, left = column(0), column(1), column(-1)
        bands = []
        for b in range(BANDS):
            mix = jnp.where(clane // CT == (b + 1) % 4, right, jnp.where(clane // CT == (b + 3) % 4, left, mine))
            bands.append(roll(mix, -CT * b, 1) * mask)
        means.append(bands)
    grad_r = [0.5 * next_minus_prev(x, 0) for x in means[1]]
    grad_c = [0.5 * next_minus_prev(x, 1) for x in means[1]]
    off = [means[1][b] - means[0][b] for b in range(BANDS)]
    now = [jnp.zeros((CROWS, 128), F32)] * 2
    bar = now
    dual_r, dual_c = list(now), list(now)
    data = [jnp.zeros((CROWS, 128), F32)] * BANDS
    for it in range(3):
        div = [0.0, 0.0]
        if it > 0:
            for c in range(2):
                pr = dual_r[c] + (0.5 * SIGMA) * next_minus_prev(bar[c], 0)
                pc = dual_c[c] + (0.5 * SIGMA) * next_minus_prev(bar[c], 1)
                k = shrink(pr * pr + pc * pc) * mask
                dual_r[c], dual_c[c] = pr * k, pc * k
                div[c] = 0.5 * (next_minus_prev(dual_r[c], 0) + next_minus_prev(dual_c[c], 1))
        pull = [0.0, 0.0]
        for b in range(BANDS):
            rho = off[b]
            if it > 0:
                rho = rho + grad_r[b] * bar[0] + grad_c[b] * bar[1]
            data[b] = jnp.clip(data[b] + SIGMA * rho, -LAM, LAM)
            pull = [pull[0] + data[b] * grad_r[b], pull[1] + data[b] * grad_c[b]]
        later = [(now[c] + TAU * (div[c] - pull[c])) * mask for c in range(2)]
        bar = [2.0 * later[c] - now[c] for c in range(2)]
        now = later
    for c in range(2):
        coarse_ref[c] = now[c][8:8 + CT, 0:CT]

    wide_shape = (128, 128 * PANELS)
    wide = lax.broadcasted_iota(jnp.int32, wide_shape, 1)
    source = jnp.where(wide < T + 64, wide // FACTOR, 128 - (128 * PANELS - wide + FACTOR - 1) // FACTOR)
    spread = jnp.where(lax.broadcasted_iota(jnp.int32, wide_shape, 0) == source, 1.0, 0.0).astype(BF16)
    block_lane = lax.broadcasted_iota(jnp.int32, (PANELS, CROWS, 128), 2)
    block_lane = block_lane + 128 * lax.broadcasted_iota(jnp.int32, (PANELS, CROWS, 128), 0)
    block_row = lax.broadcasted_iota(jnp.int32, (PANELS, CROWS, 128), 1) - 8 + me_r * CT
    block_col = jnp.where(block_lane < T + 64, block_lane, block_lane - 128 * PANELS) + me_c * T
    block_mask = jnp.where(
        (block_row >= 0) & (block_row < n_r * CT) & (block_col >= 0) & (block_col < n_c * T), 1.0, 0.0
    )
    for c in range(2):
        repeated = dot_split(now[c], spread, 3)
        t = jnp.stack([repeated[:, 128 * k:128 * k + 128] for k in range(PANELS)])
        first_r = t - roll(t, 1, 1)
        last_r = roll(t, -1, 1) - t
        step_c = across(t)
        square = step_c * step_c
        k_first = shrink(first_r * first_r + square) * block_mask
        k_inner = shrink(square) * block_mask
        k_last = shrink(last_r * last_r + square) * block_mask
        pr_first, pr_last = first_r * k_first, last_r * k_last
        pc_first, pc_inner, pc_last = step_c * k_first, step_c * k_inner, step_c * k_last
        inner = across(pc_inner)
        for n, value in enumerate((
            t, pr_first, pr_last, pc_first, pc_inner, pc_last,
            across(pc_first) - roll(pr_last, 1, 1), inner - pr_first, inner, inner + pr_last,
            across(pc_last) + roll(pr_first, -1, 1),
        )):
            tc[n, c] = value

    def block_row_of(n, c, s):
        return jnp.broadcast_to(tc[n, c, :, pl.ds(s + 7, 1), :], (PANELS, 8, 128))

    panel_sub = lax.broadcasted_iota(jnp.int32, (PANELS, 8, 128), 1)
    right_in = jnp.where(me_c == n_c - 1, 0.0, 1.0)
    left_in = jnp.where(me_c == 0, 0.0, 1.0)
    col_mask = jnp.where(panel_lane[:1] < 64, right_in, left_in)

    def inside_cols(x):
        return jnp.concatenate([x[:2], x[2:] * col_mask], axis=0)

    def clear_rows(ref):
        @pl.when(me_r == 0)
        def _():
            ref[:, :, FIRST:FIRST + 8, :] = jnp.zeros((2, PANELS, 8, 128), F32)

        @pl.when(me_r == n_r - 1)
        def _():
            ref[:, :, OFF + T:OFF + T + 8, :] = jnp.zeros((2, PANELS, 8, 128), F32)

    def opening(s, carry):
        rows = aligned(FIRST + 8 * s)
        for c in range(2):
            t, pr_first, pr_last, pc_first, pc_inner, pc_last, d0, d1, dm, d6, d7 = [
                block_row_of(n, c, s) for n in range(11)
            ]
            at0, at7 = panel_sub == 0, panel_sub == 7
            div = jnp.where(at0, d0, jnp.where(at7, d7, jnp.where(panel_sub == 1, d1, jnp.where(panel_sub == 6, d6, dm))))
            prv[c, :, rows, :] = jnp.where(at0, pr_first, jnp.where(at7, pr_last, 0.0))
            pcv[c, :, rows, :] = jnp.where(at0, pc_first, jnp.where(at7, pc_last, pc_inner))
            later = t + (1.0 / 64.0) * (div - p1[c, :, rows, :])
            u[c, :, rows, :] = later
            ub[c, :, rows, :] = inside_cols(2.0 * later - t)
        return carry

    lax.fori_loop(0, STRIPS, opening, 0, unroll=UNROLL)
    clear_rows(ub)

    for it in (1, 2):
        def dual(s, carry):
            base = FIRST + 8 * s
            rows = aligned(base)
            for c in range(2):
                pr = prv[c, :, rows, :] + (ub[c, :, pl.ds(base + 1, 8), :] - ub[c, :, pl.ds(base - 1, 8), :])
                pc = pcv[c, :, rows, :] + across(ub[c, :, rows, :])
                k = inside_cols(shrink(pr * pr + pc * pc))
                prv[c, :, rows, :] = pr * k
                pcv[c, :, rows, :] = pc * k
            return carry

        lax.fori_loop(0, STRIPS, dual, 0, unroll=UNROLL)
        clear_rows(prv)

        def primal(s, carry):
            base = FIRST + 8 * s
            rows = aligned(base)
            n = PANELS if it < 2 else 2
            step = [(ub[c, :, rows, :] - block_row_of(0, c, s))[:n] for c in range(2)]
            pull = [0.0, 0.0]
            for b in range(BANDS):
                gr, gc = g[b, 0:n, rows, :], g[BANDS + b, 0:n, rows, :]
                value = a[b, 0:n, rows, :] + gr * step[0] + gc * step[1]
                if it == 2:
                    value = value + g[2 * BANDS + b, 0:n, rows, :]
                value = jnp.clip(value, -LAM, LAM)
                if it < 2:
                    a[b, :, rows, :] = value
                pull = [pull[0] + value * gr, pull[1] + value * gc]
            for c in range(2):
                div = (
                    prv[c, 0:n, pl.ds(base + 1, 8), :] - prv[c, 0:n, pl.ds(base - 1, 8), :]
                    + across(pcv[c, :, rows, :])[:n]
                )
                was = u[c, 0:n, rows, :]
                later = was + (1.0 / 64.0) * (div - pull[c])
                if it < 2:
                    u[c, :, rows, :] = later
                    ub[c, :, rows, :] = inside_cols(2.0 * later - was)
                else:
                    for k in range(2):
                        flow_ref[c, aligned(base - OFF), 128 * k:128 * k + 128] = 8.0 * later[k]
            return carry

        if it < 2:
            lax.fori_loop(0, STRIPS, primal, 0, unroll=UNROLL)
            clear_rows(ub)
        else:
            lax.fori_loop(1, STRIPS - 1, primal, 0, unroll=8)


def local(frame_first, frame_second, shifts):
    vmem = pltpu.VMEM
    field = vmem((2, PANELS, ROWS, 128), F32)
    return pl.pallas_call(
        kernel,
        out_shape=(
            jax.ShapeDtypeStruct((2, T, T), F32),
            jax.ShapeDtypeStruct((2, CT, CT), F32),
        ),
        in_specs=[
            pl.BlockSpec(memory_space=pl.ANY),
            pl.BlockSpec(memory_space=pl.ANY),
            pl.BlockSpec(memory_space=pltpu.SMEM),
        ],
        out_specs=(pl.BlockSpec(memory_space=vmem), pl.BlockSpec(memory_space=vmem)),
        scratch_shapes=[
            vmem((BANDS, PANELS, ROWS, 128), F32),
            vmem((BANDS, 2, ROWS, 128), F32),
            vmem((3 * BANDS, PANELS, ROWS, 128), F32),
            vmem((BANDS, PANELS, ROWS, 128), F32),
            field, field, field, field, field,
            vmem((11, 2, PANELS, CROWS, 128), F32),
            vmem((2, CROWS, 128), F32),
            vmem((2, 16, 128), F32),
            vmem((8, 16, 128), F32),
            vmem((T, 128), F32),
            vmem((2, T // 2, 128), F32),
            vmem((2, T // 2, 128), F32),
            vmem((8, 16, 128), F32),
            vmem((ROWS, 128), F32),
            vmem((ROWS, 128), F32),
            vmem((8, 128), jnp.int32),
            vmem((8, 8, 128), jnp.int32),
            pltpu.SemaphoreType.DMA((4,)),
            pltpu.SemaphoreType.DMA((32,)),
            pltpu.SemaphoreType.DMA((32,)),
        ],
        compiler_params=pltpu.CompilerParams(
            collective_id=0, has_side_effects=True, vmem_limit_bytes=62 * 1024 * 1024
        ),
    )(frame_first, frame_second, shifts)


def solution(mesh):
    return jax.shard_map(
        local,
        mesh=mesh,
        in_specs=(P(None, "row", "col"), P(None, "row", "col"), P("row", "col", None)),
        out_specs=(P(None, "row", "col"), P(None, "row", "col")),
        check_vma=False,
    )
```

```python
import jax
import jax.numpy as jnp
from jax import lax
from jax.experimental import pallas as pl
from jax.experimental.pallas import tpu as pltpu
from jax.sharding import PartitionSpec as P

FACTOR = 8
TAU = 0.25
SIGMA = 0.25
LAM = 0.3
ALPHA = 0.3
BANDS = 4
T = 256
CT = T // FACTOR
OFF = 24
ROWS = T + 2 * OFF
FIRST = OFF - 8
STRIPS = T // 8 + 2
UNROLL = STRIPS // 2
MOVE = 17
PANELS = 3
DEEP = 9
THIN = 4
CROWS = CT + 16
F32 = jnp.float32
BF16 = jnp.bfloat16
DIRECTIONS = [(-1, -1), (-1, 1), (1, -1), (1, 1), (0, -1), (0, 1), (-1, 0), (1, 0)]


def split3(x):
    hi = x.astype(BF16)
    rest = x - hi.astype(F32)
    mid = rest.astype(BF16)
    low = (rest - mid.astype(F32)).astype(BF16)
    return hi, mid, low


def dot_split(x, w, parts):
    total = None
    for piece in split3(x)[:parts]:
        term = jnp.dot(piece, w, preferred_element_type=F32)
        total = term if total is None else total + term
    return total


def roll(x, amount, axis):
    amount = amount % x.shape[axis]
    return x if amount == 0 else pltpu.roll(x, amount, axis)


def next_minus_prev(x, axis):
    return roll(x, -1, axis) - roll(x, 1, axis)


def following(x):
    return jnp.concatenate([x[1:], x[:1]], axis=0)


def preceding(x):
    return jnp.concatenate([x[-1:], x[:-1]], axis=0)


def across(x):
    lane = lax.broadcasted_iota(jnp.int32, x.shape, 2)
    ahead, behind = roll(x, -1, 2), roll(x, 1, 2)
    return jnp.where(lane == 127, following(ahead), ahead) - jnp.where(lane == 0, preceding(behind), behind)


def shrink(square):
    return jnp.minimum(1.0, ALPHA * lax.rsqrt(square))


def aligned(start, size=8):
    return pl.ds(pl.multiple_of(start, 8), size)


def kernel(
    f1_ref, f2_ref, sh_ref, flow_ref, coarse_ref,
    s2, wv, f1v, g, a, p1, u, ub, prv, pcv, tc, ce, cs, cr,
    pack, es, er, kr, eq, own, shs, shr,
    local_sem, send_sem, recv_sem,
):
    me_r, me_c = lax.axis_index("row"), lax.axis_index("col")
    n_r, n_c = lax.axis_size("row"), lax.axis_size("col")

    def device(direction):
        dr, dc = direction
        return (lax.rem(me_r + dr + n_r, n_r), lax.rem(me_c + dc + n_c, n_c))

    barrier = pltpu.get_barrier_semaphore()
    for direction in DIRECTIONS:
        pl.semaphore_signal(barrier, inc=1, device_id=device(direction), device_id_type=pl.DeviceIdType.MESH)
    gets = []
    for ref, kept in ((f2_ref, s2), (f1_ref, f1v)):
        for k in range(2):
            copy = pltpu.make_async_copy(
                ref.at[:, :, pl.ds(128 * k, 128)], kept.at[:, k, pl.ds(OFF, T), :], local_sem.at[len(gets)]
            )
            copy.start()
            gets.append(copy)
    my_shift = (sh_ref[0, 0, 0], sh_ref[0, 0, 1])
    sub8 = lax.broadcasted_iota(jnp.int32, (8, 128), 0)
    shs[...] = jnp.where(sub8 == 0, my_shift[0], my_shift[1])

    sends = []

    def send(src, dst, direction):
        slot = len(sends)
        copy = pltpu.make_async_remote_copy(
            src_ref=src, dst_ref=dst, send_sem=send_sem.at[slot], recv_sem=recv_sem.at[slot],
            device_id=device(direction), device_id_type=pl.DeviceIdType.MESH,
        )
        copy.start()
        sends.append(copy)

    lane = lax.broadcasted_iota(jnp.int32, (8, 128), 1)
    place = lane % 16
    right_side = lane < 64
    tall = lax.broadcasted_iota(jnp.int32, (T // 2, 128), 1) < 64
    for copy in gets:
        copy.wait()

    def packing(i, carry):
        rows = aligned(OFF + 8 * i)
        acc = jnp.zeros((8, 128), F32)
        for b in range(BANDS):
            left2, right2, left1, right1 = s2[b, 0, rows, :], s2[b, 1, rows, :], f1v[b, 0, rows, :], f1v[b, 1, rows, :]
            left = jnp.where(place < 6, roll(left1, 16 * b, 1), roll(left2, 16 * b + 6, 1))
            right = jnp.where(place < 10, roll(right2, 16 * b + 74, 1), roll(right1, 16 * b + 78, 1))
            acc = jnp.where(lane // 16 == b, left, jnp.where(lane // 16 == b + 4, right, acc))
        pack[aligned(8 * i), :] = acc
        return carry

    lax.fori_loop(0, T // 8, packing, 0, unroll=32)
    upper, lower = pack[0:128, :], pack[128:256, :]
    es[0] = jnp.where(tall, upper, roll(lower, 64, 1))
    es[1] = jnp.where(tall, roll(upper, 64, 1), lower)

    pl.semaphore_wait(barrier, len(DIRECTIONS))

    for dr, dc in DIRECTIONS:
        seen = DIRECTIONS.index((-dr, -dc))
        if dr != 0 and dc != 0:
            send(pack.at[pl.ds(0 if dr < 0 else T - 16, 16), :], kr.at[seen], (dr, dc))
        elif dr == 0:
            side = 0 if dc < 0 else 1
            send(es.at[side], er.at[side], (dr, dc))
        else:
            from2, to2 = (OFF, OFF + T) if dr < 0 else (OFF + T - DEEP, OFF - DEEP)
            from1, to1 = (OFF, OFF + T) if dr < 0 else (OFF + T - THIN, OFF - THIN)
            both = pl.ds(0, 2)
            send(s2.at[:, both, pl.ds(from2, DEEP), :], s2.at[:, both, pl.ds(to2, DEEP), :], (dr, dc))
            send(f1v.at[:, both, pl.ds(from1, THIN), :], f1v.at[:, both, pl.ds(to1, THIN), :], (dr, dc))
        send(shs, shr.at[seen], (dr, dc))
    raw_count = len(sends)

    col_id = lax.broadcasted_iota(jnp.int32, (128, 128), 0) // FACTOR
    lane_id = lax.broadcasted_iota(jnp.int32, (128, 128), 1)
    row_sum = (
        lax.broadcasted_iota(jnp.int32, (CT, T), 1) // FACTOR == lax.broadcasted_iota(jnp.int32, (CT, T), 0)
    ).astype(F32).astype(BF16)
    for frame in range(2):
        total = jnp.zeros((T, 128), F32)
        for b in range(BANDS):
            for k in range(2):
                block = (f1v if frame == 0 else s2)[b, k, OFF:OFF + T, :]
                weights = jnp.where(lane_id - CT * b - 16 * k == col_id, 1.0 / 64.0, 0.0).astype(BF16)
                total = total + dot_split(block, weights, 2)
        hi, mid, _ = split3(total)
        ce[frame, 8:8 + CT, :] = (
            jnp.dot(row_sum, hi, preferred_element_type=F32) + jnp.dot(row_sum, mid, preferred_element_type=F32)
        )
    group = (lax.broadcasted_iota(jnp.int32, (16, 128), 1) % CT) // 8
    edge_l = edge_r = jnp.zeros((16, 128), F32)
    for frame in range(2):
        for half in range(2):
            n = 2 * frame + half
            piece = ce[frame, 8 + 16 * half:24 + 16 * half, :]
            edge_l = jnp.where(group == n, roll(piece, 8 * n, 1), edge_l)
            edge_r = jnp.where(group == n, roll(piece, 8 * n - 24, 1), edge_r)
    for half in range(2):
        cs[0, half] = edge_l[8 * half:8 * half + 8]
        cs[1, half] = edge_r[8 * half:8 * half + 8]

    for dr, dc in DIRECTIONS:
        seen = DIRECTIONS.index((-dr, -dc))
        if dr == 0:
            send(cs.at[0 if dc < 0 else 1], cr.at[seen], (dr, dc))
        else:
            send(ce.at[:, pl.ds(8 if dr < 0 else CT, 8), :], cr.at[seen], (dr, dc))

    def own_edge(start):
        acc = jnp.zeros((8, 128), F32)
        for b in range(BANDS):
            left, right = s2[b, 0, aligned(start), :], s2[b, 1, aligned(start), :]
            acc = jnp.where(lane // 16 == b, roll(right, 16 * b + 6, 1), acc)
            acc = jnp.where(lane // 16 == b + 4, roll(left, 16 * b + 74, 1), acc)
        return acc

    def owning(i, carry):
        own[aligned(OFF + 8 * i), :] = own_edge(OFF + 8 * i)
        return carry

    lax.fori_loop(0, T // 8, owning, 0, unroll=8)

    for copy in sends[:raw_count]:
        copy.wait()

    def at(direction):
        return DIRECTIONS.index(direction)

    shift_at = {d: (shr[at(d), 0, 0], shr[at(d), 1, 0]) for d in DIRECTIONS}

    keep_lane = jnp.where(
        lane[0:1] < 64, jnp.where(me_c == n_c - 1, 0.0, 1.0), jnp.where(me_c == 0, 0.0, 1.0)
    )
    eq[OFF:OFF + 128, :] = jnp.where(tall, er[0], roll(er[1], 64, 1)) * keep_lane
    eq[OFF + 128:OFF + 256, :] = jnp.where(tall, roll(er[0], 64, 1), er[1]) * keep_lane
    side16 = lax.broadcasted_iota(jnp.int32, (16, 128), 1) < 64
    eq[OFF - 16:OFF, :] = jnp.where(side16, kr[at((-1, 1))], kr[at((-1, -1))]) * keep_lane
    eq[OFF + T:OFF + T + 16, :] = jnp.where(side16, kr[at((1, 1))], kr[at((1, -1))]) * keep_lane

    @pl.when(me_r == 0)
    def _():
        s2[:, 0:2, OFF - 16:OFF, :] = jnp.zeros((BANDS, 2, 16, 128), F32)
        eq[OFF - 16:OFF, :] = jnp.zeros((16, 128), F32)

    @pl.when(me_r == n_r - 1)
    def _():
        s2[:, 0:2, OFF + T:OFF + T + 16, :] = jnp.zeros((BANDS, 2, 16, 128), F32)
        eq[OFF + T:OFF + T + 16, :] = jnp.zeros((16, 128), F32)

    for start in (OFF - 16, OFF - 8, OFF + T, OFF + T + 8):
        own[start:start + 8, :] = own_edge(start)

    theirs = (right_side & (place >= 6)) | ((lane >= 64) & (place < 10))

    def third(i, carry):
        rows = aligned(OFF - 16 + 8 * i)
        x = eq[rows, :]
        mix = jnp.where((place >= 6) & (place < 13), x, roll(x, 60, 1))
        for b in range(BANDS):
            s2[b, 2, rows, :] = roll(mix, -(16 * b + 6), 1)
        own[rows, :] = jnp.where(theirs, x, own[rows, :])
        return carry

    lax.fori_loop(0, STRIPS + 2, third, 0, unroll=18)

    panel_lane = lax.broadcasted_iota(jnp.int32, (PANELS, 8, 128), 2)

    def back(shift):
        return jnp.where(shift > 0, 128 - shift, -shift)

    def store_data(fields, b, panels, rows, pull):
        dr, dc, wf = fields
        first = jnp.clip(wf, -LAM, LAM)
        g[b, panels, rows, :] = dr
        g[BANDS + b, panels, rows, :] = dc
        g[2 * BANDS + b, panels, rows, :] = wf
        a[b, panels, rows, :] = first + wf
        return [pull[0] + first * dr, pull[1] + first * dc]

    def window(base, shift):
        rows = aligned(base)
        start = base + shift[0]
        amount = back(shift[1])
        over = panel_lane + shift[1] >= 128
        under = panel_lane + shift[1] < 0

        def shifted(x):
            turned = pltpu.roll(x, amount, 2)
            return jnp.where(over, following(turned), jnp.where(under, preceding(turned), turned))

        pull = [0.0, 0.0]
        for b in range(BANDS):
            here = shifted(s2[b, :, pl.ds(start, 8), :])
            down = shifted(s2[b, :, pl.ds(start + 1, 8), :] - s2[b, :, pl.ds(start - 1, 8), :])
            fields = (down[:2], across(here)[:2], SIGMA * (here[:2] - f1v[b, :, rows, :]))
            pull = store_data(fields, b, slice(0, 2), rows, pull)
        for c in range(2):
            p1[c, 0:2, rows, :] = pull[c]

    amount = back(my_shift[1])
    over = panel_lane + my_shift[1] >= 128
    under = panel_lane + my_shift[1] < 0

    def moving(s, carry):
        base = FIRST + 8 * s
        for b in range(BANDS):
            turned = pltpu.roll(s2[b, :, pl.ds(base + my_shift[0], 8), :], amount, 2)
            wv[b, :, aligned(base), :] = jnp.where(
                over, following(turned), jnp.where(under, preceding(turned), turned)
            )
        return carry

    lax.fori_loop(0, STRIPS, moving, 0, unroll=MOVE)

    def window_loop(i, carry):
        base = OFF + 8 * i
        rows = aligned(base)
        pull = [0.0, 0.0]
        for b in range(BANDS):
            here = wv[b, :, rows, :]
            fields = (
                wv[b, 0:2, pl.ds(base + 1, 8), :] - wv[b, 0:2, pl.ds(base - 1, 8), :],
                across(here)[:2],
                SIGMA * (here[:2] - f1v[b, :, rows, :]),
            )
            pull = store_data(fields, b, slice(0, 2), rows, pull)
        for c in range(2):
            p1[c, 0:2, rows, :] = pull[c]
        return carry

    lax.fori_loop(0, T // 8, window_loop, 0, unroll=4)
    window(OFF - 8, shift_at[(-1, 0)])
    window(OFF + T, shift_at[(1, 0)])

    def edge(base, right, left):
        rows = aligned(base)

        def pick(x, y):
            return jnp.where(right_side, pltpu.roll(x, back(right[1]), 1), pltpu.roll(y, back(left[1]), 1))

        def near(shift, step):
            return own[pl.ds(base + shift[0] + step, 8), :]

        here = pick(near(right, 0), near(left, 0))
        down = pick(near(right, 1) - near(right, -1), near(left, 1) - near(left, -1))
        x = eq[rows, :]
        first = jnp.where(right_side, roll(x, 6, 1), roll(x, -4, 1))
        kinds = []
        for field in (down, next_minus_prev(here, 1), SIGMA * (here - first)):
            kinds.append(jnp.where((place >= 6) & (place < 10), field, roll(field, 60, 1)))
        pull = [0.0, 0.0]
        for b in range(BANDS):
            fields = [roll(kind, -(16 * b + 6), 1) for kind in kinds]
            pull = store_data(fields, b, 2, rows, pull)
        for c in range(2):
            p1[c, 2, rows, :] = pull[c]

    def edge_loop(i, carry):
        edge(OFF + 8 * i, shift_at[(0, 1)], shift_at[(0, -1)])
        return carry

    lax.fori_loop(0, T // 8, edge_loop, 0, unroll=8)
    edge(OFF - 8, shift_at[(-1, 1)], shift_at[(-1, -1)])
    edge(OFF + T, shift_at[(1, 1)], shift_at[(1, -1)])

    crow = lax.broadcasted_iota(jnp.int32, (CROWS, 128), 0) - 8 + me_r * CT
    clane = lax.broadcasted_iota(jnp.int32, (CROWS, 128), 1)
    ccol = jnp.where(clane < 64, clane, clane - 128) + me_c * CT
    mask = jnp.where((crow >= 0) & (crow < n_r * CT) & (ccol >= 0) & (ccol < n_c * CT), 1.0, 0.0)
    for copy in sends[raw_count:]:
        copy.wait()
    means = []
    for frame in range(2):
        def column(dc):
            parts = [cr[at((-1, dc)), frame]]
            turn = CT * dc
            if dc == 0:
                parts.append(ce[frame, 8:8 + CT, :])
            else:
                for half in range(2):
                    n = 2 * frame + half
                    side = cr[at((0, dc))]
                    side = jnp.concatenate([side[0], side[1]], axis=0)
                    parts.append(roll(side, (0 if dc > 0 else 24) - 8 * n, 1))
            parts.append(cr[at((1, dc)), frame])
            return roll(jnp.concatenate(parts, axis=0), turn, 1)

        mine, right, left = column(0), column(1), column(-1)
        bands = []
        for b in range(BANDS):
            mix = jnp.where(clane // CT == (b + 1) % 4, right, jnp.where(clane // CT == (b + 3) % 4, left, mine))
            bands.append(roll(mix, -CT * b, 1) * mask)
        means.append(bands)
    grad_r = [0.5 * next_minus_prev(x, 0) for x in means[1]]
    grad_c = [0.5 * next_minus_prev(x, 1) for x in means[1]]
    off = [means[1][b] - means[0][b] for b in range(BANDS)]
    now = [jnp.zeros((CROWS, 128), F32)] * 2
    bar = now
    dual_r, dual_c = list(now), list(now)
    data = [jnp.zeros((CROWS, 128), F32)] * BANDS
    for it in range(3):
        div = [0.0, 0.0]
        if it > 0:
            for c in range(2):
                pr = dual_r[c] + (0.5 * SIGMA) * next_minus_prev(bar[c], 0)
                pc = dual_c[c] + (0.5 * SIGMA) * next_minus_prev(bar[c], 1)
                k = shrink(pr * pr + pc * pc) * mask
                dual_r[c], dual_c[c] = pr * k, pc * k
                div[c] = 0.5 * (next_minus_prev(dual_r[c], 0) + next_minus_prev(dual_c[c], 1))
        pull = [0.0, 0.0]
        for b in range(BANDS):
            rho = off[b]
            if it > 0:
                rho = rho + grad_r[b] * bar[0] + grad_c[b] * bar[1]
            data[b] = jnp.clip(data[b] + SIGMA * rho, -LAM, LAM)
            pull = [pull[0] + data[b] * grad_r[b], pull[1] + data[b] * grad_c[b]]
        later = [(now[c] + TAU * (div[c] - pull[c])) * mask for c in range(2)]
        bar = [2.0 * later[c] - now[c] for c in range(2)]
        now = later
    for c in range(2):
        coarse_ref[c] = now[c][8:8 + CT, 0:CT]

    wide_shape = (128, 128 * PANELS)
    wide = lax.broadcasted_iota(jnp.int32, wide_shape, 1)
    source = jnp.where(wide < T + 64, wide // FACTOR, 128 - (128 * PANELS - wide + FACTOR - 1) // FACTOR)
    spread = jnp.where(lax.broadcasted_iota(jnp.int32, wide_shape, 0) == source, 1.0, 0.0).astype(BF16)
    block_lane = lax.broadcasted_iota(jnp.int32, (PANELS, CROWS, 128), 2)
    block_lane = block_lane + 128 * lax.broadcasted_iota(jnp.int32, (PANELS, CROWS, 128), 0)
    block_row = lax.broadcasted_iota(jnp.int32, (PANELS, CROWS, 128), 1) - 8 + me_r * CT
    block_col = jnp.where(block_lane < T + 64, block_lane, block_lane - 128 * PANELS) + me_c * T
    block_mask = jnp.where(
        (block_row >= 0) & (block_row < n_r * CT) & (block_col >= 0) & (block_col < n_c * T), 1.0, 0.0
    )
    for c in range(2):
        repeated = dot_split(now[c], spread, 3)
        t = jnp.stack([repeated[:, 128 * k:128 * k + 128] for k in range(PANELS)])
        first_r = t - roll(t, 1, 1)
        last_r = roll(t, -1, 1) - t
        step_c = across(t)
        square = step_c * step_c
        k_first = shrink(first_r * first_r + square) * block_mask
        k_inner = shrink(square) * block_mask
        k_last = shrink(last_r * last_r + square) * block_mask
        pr_first, pr_last = first_r * k_first, last_r * k_last
        pc_first, pc_inner, pc_last = step_c * k_first, step_c * k_inner, step_c * k_last
        inner = across(pc_inner)
        for n, value in enumerate((
            t, pr_first, pr_last, pc_first, pc_inner, pc_last,
            across(pc_first) - roll(pr_last, 1, 1), inner - pr_first, inner, inner + pr_last,
            across(pc_last) + roll(pr_first, -1, 1),
        )):
            tc[n, c] = value

    def block_row_of(n, c, s):
        return jnp.broadcast_to(tc[n, c, :, pl.ds(s + 7, 1), :], (PANELS, 8, 128))

    panel_sub = lax.broadcasted_iota(jnp.int32, (PANELS, 8, 128), 1)
    right_in = jnp.where(me_c == n_c - 1, 0.0, 1.0)
    left_in = jnp.where(me_c == 0, 0.0, 1.0)
    col_mask = jnp.where(panel_lane[:1] < 64, right_in, left_in)

    def inside_cols(x):
        return jnp.concatenate([x[:2], x[2:] * col_mask], axis=0)

    def clear_rows(ref):
        @pl.when(me_r == 0)
        def _():
            ref[:, :, FIRST:FIRST + 8, :] = jnp.zeros((2, PANELS, 8, 128), F32)

        @pl.when(me_r == n_r - 1)
        def _():
            ref[:, :, OFF + T:OFF + T + 8, :] = jnp.zeros((2, PANELS, 8, 128), F32)

    def opening(s, carry):
        rows = aligned(FIRST + 8 * s)
        for c in range(2):
            t, pr_first, pr_last, pc_first, pc_inner, pc_last, d0, d1, dm, d6, d7 = [
                block_row_of(n, c, s) for n in range(11)
            ]
            at0, at7 = panel_sub == 0, panel_sub == 7
            div = jnp.where(at0, d0, jnp.where(at7, d7, jnp.where(panel_sub == 1, d1, jnp.where(panel_sub == 6, d6, dm))))
            prv[c, :, rows, :] = jnp.where(at0, pr_first, jnp.where(at7, pr_last, 0.0))
            pcv[c, :, rows, :] = jnp.where(at0, pc_first, jnp.where(at7, pc_last, pc_inner))
            later = t + (1.0 / 64.0) * (div - p1[c, :, rows, :])
            u[c, :, rows, :] = later
            ub[c, :, rows, :] = inside_cols(2.0 * later - t)
        return carry

    lax.fori_loop(0, STRIPS, opening, 0, unroll=UNROLL)
    clear_rows(ub)

    for it in (1, 2):
        def dual(s, carry):
            base = FIRST + 8 * s
            rows = aligned(base)
            for c in range(2):
                pr = prv[c, :, rows, :] + (ub[c, :, pl.ds(base + 1, 8), :] - ub[c, :, pl.ds(base - 1, 8), :])
                pc = pcv[c, :, rows, :] + across(ub[c, :, rows, :])
                k = inside_cols(shrink(pr * pr + pc * pc))
                prv[c, :, rows, :] = pr * k
                pcv[c, :, rows, :] = pc * k
            return carry

        lax.fori_loop(0, STRIPS, dual, 0, unroll=UNROLL)
        clear_rows(prv)

        def primal(s, carry):
            base = FIRST + 8 * s
            rows = aligned(base)
            n = PANELS if it < 2 else 2
            step = [(ub[c, :, rows, :] - block_row_of(0, c, s))[:n] for c in range(2)]
            pull = [0.0, 0.0]
            for b in range(BANDS):
                gr, gc = g[b, 0:n, rows, :], g[BANDS + b, 0:n, rows, :]
                value = a[b, 0:n, rows, :] + gr * step[0] + gc * step[1]
                if it == 2:
                    value = value + g[2 * BANDS + b, 0:n, rows, :]
                value = jnp.clip(value, -LAM, LAM)
                if it < 2:
                    a[b, :, rows, :] = value
                pull = [pull[0] + value * gr, pull[1] + value * gc]
            for c in range(2):
                div = (
                    prv[c, 0:n, pl.ds(base + 1, 8), :] - prv[c, 0:n, pl.ds(base - 1, 8), :]
                    + across(pcv[c, :, rows, :])[:n]
                )
                was = u[c, 0:n, rows, :]
                later = was + (1.0 / 64.0) * (div - pull[c])
                if it < 2:
                    u[c, :, rows, :] = later
                    ub[c, :, rows, :] = inside_cols(2.0 * later - was)
                else:
                    for k in range(2):
                        flow_ref[c, aligned(base - OFF), 128 * k:128 * k + 128] = 8.0 * later[k]
            return carry

        if it < 2:
            lax.fori_loop(0, STRIPS, primal, 0, unroll=UNROLL)
            clear_rows(ub)
        else:
            lax.fori_loop(1, STRIPS - 1, primal, 0, unroll=8)


def local(frame_first, frame_second, shifts):
    vmem = pltpu.VMEM
    field = vmem((2, PANELS, ROWS, 128), F32)
    return pl.pallas_call(
        kernel,
        out_shape=(
            jax.ShapeDtypeStruct((2, T, T), F32),
            jax.ShapeDtypeStruct((2, CT, CT), F32),
        ),
        in_specs=[
            pl.BlockSpec(memory_space=pl.ANY),
            pl.BlockSpec(memory_space=pl.ANY),
            pl.BlockSpec(memory_space=pltpu.SMEM),
        ],
        out_specs=(pl.BlockSpec(memory_space=vmem), pl.BlockSpec(memory_space=vmem)),
        scratch_shapes=[
            vmem((BANDS, PANELS, ROWS, 128), F32),
            vmem((BANDS, PANELS, ROWS, 128), F32),
            vmem((BANDS, 2, ROWS, 128), F32),
            vmem((3 * BANDS, PANELS, ROWS, 128), F32),
            vmem((BANDS, PANELS, ROWS, 128), F32),
            field, field, field, field, field,
            vmem((11, 2, PANELS, CROWS, 128), F32),
            vmem((2, CROWS, 128), F32),
            vmem((2, 2, 8, 128), F32),
            vmem((8, 2, 8, 128), F32),
            vmem((T, 128), F32),
            vmem((2, T // 2, 128), F32),
            vmem((2, T // 2, 128), F32),
            vmem((8, 16, 128), F32),
            vmem((ROWS, 128), F32),
            vmem((ROWS, 128), F32),
            vmem((8, 128), jnp.int32),
            vmem((8, 8, 128), jnp.int32),
            pltpu.SemaphoreType.DMA((4,)),
            pltpu.SemaphoreType.DMA((32,)),
            pltpu.SemaphoreType.DMA((32,)),
        ],
        compiler_params=pltpu.CompilerParams(
            collective_id=0, has_side_effects=True, vmem_limit_bytes=62 * 1024 * 1024
        ),
    )(frame_first, frame_second, shifts)


def solution(mesh):
    return jax.shard_map(
        local,
        mesh=mesh,
        in_specs=(P(None, "row", "col"), P(None, "row", "col"), P("row", "col", None)),
        out_specs=(P(None, "row", "col"), P(None, "row", "col")),
        check_vma=False,
    )
```

```python
import jax
import jax.numpy as jnp
from jax import lax
from jax.experimental import pallas as pl
from jax.experimental.pallas import tpu as pltpu
from jax.sharding import PartitionSpec as P

FACTOR = 8
TAU = 0.25
SIGMA = 0.25
LAM = 0.3
ALPHA = 0.3
BANDS = 4
T = 256
CT = T // FACTOR
OFF = 24
ROWS = T + 2 * OFF
FIRST = OFF - 8
STRIPS = T // 8 + 2
UNROLL = STRIPS // 2
MOVE = 16
EDGE = 10
PANELS = 3
DEEP = 9
THIN = 4
CROWS = CT + 16
F32 = jnp.float32
BF16 = jnp.bfloat16
DIRECTIONS = [(-1, -1), (-1, 1), (1, -1), (1, 1), (0, -1), (0, 1), (-1, 0), (1, 0)]


def split3(x):
    hi = x.astype(BF16)
    rest = x - hi.astype(F32)
    mid = rest.astype(BF16)
    low = (rest - mid.astype(F32)).astype(BF16)
    return hi, mid, low


def dot_split(x, w, parts):
    total = None
    for piece in split3(x)[:parts]:
        term = jnp.dot(piece, w, preferred_element_type=F32)
        total = term if total is None else total + term
    return total


def roll(x, amount, axis):
    amount = amount % x.shape[axis]
    return x if amount == 0 else pltpu.roll(x, amount, axis)


def next_minus_prev(x, axis):
    return roll(x, -1, axis) - roll(x, 1, axis)


def following(x):
    return jnp.concatenate([x[1:], x[:1]], axis=0)


def preceding(x):
    return jnp.concatenate([x[-1:], x[:-1]], axis=0)


def across(x):
    lane = lax.broadcasted_iota(jnp.int32, x.shape, 2)
    ahead, behind = roll(x, -1, 2), roll(x, 1, 2)
    return jnp.where(lane == 127, following(ahead), ahead) - jnp.where(lane == 0, preceding(behind), behind)


def shrink(square):
    return jnp.minimum(1.0, ALPHA * lax.rsqrt(square))


def aligned(start, size=8):
    return pl.ds(pl.multiple_of(start, 8), size)


def kernel(
    f1_ref, f2_ref, sh_ref, flow_ref, coarse_ref,
    s2, wv, f1v, g, a, p1, u, ub, prv, pcv, tc, ce, cs, cr,
    pack, es, er, kr, eq, own, shs, shr,
    local_sem, send_sem, recv_sem,
):
    me_r, me_c = lax.axis_index("row"), lax.axis_index("col")
    n_r, n_c = lax.axis_size("row"), lax.axis_size("col")

    def device(direction):
        dr, dc = direction
        return (lax.rem(me_r + dr + n_r, n_r), lax.rem(me_c + dc + n_c, n_c))

    barrier = pltpu.get_barrier_semaphore()
    for direction in DIRECTIONS:
        pl.semaphore_signal(barrier, inc=1, device_id=device(direction), device_id_type=pl.DeviceIdType.MESH)
    gets = []
    for ref, kept in ((f2_ref, s2), (f1_ref, f1v)):
        for k in range(2):
            copy = pltpu.make_async_copy(
                ref.at[:, :, pl.ds(128 * k, 128)], kept.at[:, k, pl.ds(OFF, T), :], local_sem.at[len(gets)]
            )
            copy.start()
            gets.append(copy)
    my_shift = (sh_ref[0, 0, 0], sh_ref[0, 0, 1])
    sub8 = lax.broadcasted_iota(jnp.int32, (8, 128), 0)
    shs[...] = jnp.where(sub8 == 0, my_shift[0], my_shift[1])

    sends = []

    def send(src, dst, direction):
        slot = len(sends)
        copy = pltpu.make_async_remote_copy(
            src_ref=src, dst_ref=dst, send_sem=send_sem.at[slot], recv_sem=recv_sem.at[slot],
            device_id=device(direction), device_id_type=pl.DeviceIdType.MESH,
        )
        copy.start()
        sends.append((copy, direction[0] != 0 and direction[1] != 0))

    lane = lax.broadcasted_iota(jnp.int32, (8, 128), 1)
    place = lane % 16
    right_side = lane < 64
    tall = lax.broadcasted_iota(jnp.int32, (T // 2, 128), 1) < 64
    for copy in gets:
        copy.wait()

    def packing(i, carry):
        rows = aligned(OFF + 8 * i)
        acc = jnp.zeros((8, 128), F32)
        for b in range(BANDS):
            left2, right2, left1, right1 = s2[b, 0, rows, :], s2[b, 1, rows, :], f1v[b, 0, rows, :], f1v[b, 1, rows, :]
            left = jnp.where(place < 6, roll(left1, 16 * b, 1), roll(left2, 16 * b + 6, 1))
            right = jnp.where(place < 10, roll(right2, 16 * b + 74, 1), roll(right1, 16 * b + 78, 1))
            acc = jnp.where(lane // 16 == b, left, jnp.where(lane // 16 == b + 4, right, acc))
        pack[aligned(8 * i), :] = acc
        return carry

    lax.fori_loop(0, T // 8, packing, 0, unroll=32)
    upper, lower = pack[0:128, :], pack[128:256, :]
    es[0] = jnp.where(tall, upper, roll(lower, 64, 1))
    es[1] = jnp.where(tall, roll(upper, 64, 1), lower)

    pl.semaphore_wait(barrier, len(DIRECTIONS))

    for dr, dc in DIRECTIONS:
        seen = DIRECTIONS.index((-dr, -dc))
        if dr != 0 and dc != 0:
            send(pack.at[pl.ds(0 if dr < 0 else T - 16, 16), :], kr.at[seen], (dr, dc))
        elif dr == 0:
            side = 0 if dc < 0 else 1
            send(es.at[side], er.at[side], (dr, dc))
        else:
            from2, to2 = (OFF, OFF + T) if dr < 0 else (OFF + T - DEEP, OFF - DEEP)
            from1, to1 = (OFF, OFF + T) if dr < 0 else (OFF + T - THIN, OFF - THIN)
            both = pl.ds(0, 2)
            send(s2.at[:, both, pl.ds(from2, DEEP), :], s2.at[:, both, pl.ds(to2, DEEP), :], (dr, dc))
            send(f1v.at[:, both, pl.ds(from1, THIN), :], f1v.at[:, both, pl.ds(to1, THIN), :], (dr, dc))
        send(shs, shr.at[seen], (dr, dc))
    raw_count = len(sends)

    col_id = lax.broadcasted_iota(jnp.int32, (128, 128), 0) // FACTOR
    lane_id = lax.broadcasted_iota(jnp.int32, (128, 128), 1)
    row_sum = (
        lax.broadcasted_iota(jnp.int32, (CT, T), 1) // FACTOR == lax.broadcasted_iota(jnp.int32, (CT, T), 0)
    ).astype(F32).astype(BF16)
    for frame in range(2):
        total = jnp.zeros((T, 128), F32)
        for b in range(BANDS):
            for k in range(2):
                block = (f1v if frame == 0 else s2)[b, k, OFF:OFF + T, :]
                weights = jnp.where(lane_id - CT * b - 16 * k == col_id, 1.0 / 64.0, 0.0).astype(BF16)
                total = total + dot_split(block, weights, 2)
        hi, mid, _ = split3(total)
        ce[frame, 8:8 + CT, :] = (
            jnp.dot(row_sum, hi, preferred_element_type=F32) + jnp.dot(row_sum, mid, preferred_element_type=F32)
        )
    group = (lax.broadcasted_iota(jnp.int32, (16, 128), 1) % CT) // 8
    edge_l = edge_r = jnp.zeros((16, 128), F32)
    for frame in range(2):
        for half in range(2):
            n = 2 * frame + half
            piece = ce[frame, 8 + 16 * half:24 + 16 * half, :]
            edge_l = jnp.where(group == n, roll(piece, 8 * n, 1), edge_l)
            edge_r = jnp.where(group == n, roll(piece, 8 * n - 24, 1), edge_r)
    for half in range(2):
        cs[0, half] = edge_l[8 * half:8 * half + 8]
        cs[1, half] = edge_r[8 * half:8 * half + 8]

    for dr, dc in DIRECTIONS:
        seen = DIRECTIONS.index((-dr, -dc))
        if dr == 0:
            send(cs.at[0 if dc < 0 else 1], cr.at[seen], (dr, dc))
        else:
            send(ce.at[:, pl.ds(8 if dr < 0 else CT, 8), :], cr.at[seen], (dr, dc))

    def own_edge(start):
        acc = jnp.zeros((8, 128), F32)
        for b in range(BANDS):
            left, right = s2[b, 0, aligned(start), :], s2[b, 1, aligned(start), :]
            acc = jnp.where(lane // 16 == b, roll(right, 16 * b + 6, 1), acc)
            acc = jnp.where(lane // 16 == b + 4, roll(left, 16 * b + 74, 1), acc)
        return acc

    def owning(i, carry):
        own[aligned(OFF + 8 * i), :] = own_edge(OFF + 8 * i)
        return carry

    lax.fori_loop(0, T // 8, owning, 0, unroll=8)

    for copy, diagonal in sends[:raw_count]:
        if not diagonal:
            copy.wait()

    def at(direction):
        return DIRECTIONS.index(direction)

    def shift_at(d):
        return shr[at(d), 0, 0], shr[at(d), 1, 0]

    keep_lane = jnp.where(
        lane[0:1] < 64, jnp.where(me_c == n_c - 1, 0.0, 1.0), jnp.where(me_c == 0, 0.0, 1.0)
    )
    eq[OFF:OFF + 128, :] = jnp.where(tall, er[0], roll(er[1], 64, 1)) * keep_lane
    eq[OFF + 128:OFF + 256, :] = jnp.where(tall, roll(er[0], 64, 1), er[1]) * keep_lane

    @pl.when(me_r == 0)
    def _():
        s2[:, 0:2, OFF - 16:OFF, :] = jnp.zeros((BANDS, 2, 16, 128), F32)

    @pl.when(me_r == n_r - 1)
    def _():
        s2[:, 0:2, OFF + T:OFF + T + 16, :] = jnp.zeros((BANDS, 2, 16, 128), F32)

    for start in (OFF - 16, OFF - 8, OFF + T, OFF + T + 8):
        own[start:start + 8, :] = own_edge(start)

    theirs = (right_side & (place >= 6)) | ((lane >= 64) & (place < 10))

    def third(i, carry):
        rows = aligned(OFF - 16 + 8 * i)
        x = eq[rows, :]
        mix = jnp.where((place >= 6) & (place < 13), x, roll(x, 60, 1))
        for b in range(BANDS):
            s2[b, 2, rows, :] = roll(mix, -(16 * b + 6), 1)
        own[rows, :] = jnp.where(theirs, x, own[rows, :])
        return carry

    lax.fori_loop(2, STRIPS, third, 0, unroll=16)

    panel_lane = lax.broadcasted_iota(jnp.int32, (PANELS, 8, 128), 2)

    def back(shift):
        return jnp.where(shift > 0, 128 - shift, -shift)

    def store_data(fields, b, panels, rows, pull):
        dr, dc, wf = fields
        first = jnp.clip(wf, -LAM, LAM)
        g[b, panels, rows, :] = dr
        g[BANDS + b, panels, rows, :] = dc
        g[2 * BANDS + b, panels, rows, :] = wf
        a[b, panels, rows, :] = first + wf
        return [pull[0] + first * dr, pull[1] + first * dc]

    def window(base, shift):
        rows = aligned(base)
        start = base + shift[0]
        amount = back(shift[1])
        over = panel_lane + shift[1] >= 128
        under = panel_lane + shift[1] < 0

        def shifted(x):
            turned = pltpu.roll(x, amount, 2)
            return jnp.where(over, following(turned), jnp.where(under, preceding(turned), turned))

        pull = [0.0, 0.0]
        for b in range(BANDS):
            here = shifted(s2[b, :, pl.ds(start, 8), :])
            down = shifted(s2[b, :, pl.ds(start + 1, 8), :] - s2[b, :, pl.ds(start - 1, 8), :])
            fields = (down[:2], across(here)[:2], SIGMA * (here[:2] - f1v[b, :, rows, :]))
            pull = store_data(fields, b, slice(0, 2), rows, pull)
        for c in range(2):
            p1[c, 0:2, rows, :] = pull[c]

    amount = back(my_shift[1])
    over = panel_lane + my_shift[1] >= 128
    under = panel_lane + my_shift[1] < 0

    def moving(s, carry):
        base = FIRST + 8 * s
        for b in range(BANDS):
            turned = pltpu.roll(s2[b, :, pl.ds(base + my_shift[0], 8), :], amount, 2)
            wv[b, :, aligned(base), :] = jnp.where(
                over, following(turned), jnp.where(under, preceding(turned), turned)
            )
        return carry

    lax.fori_loop(1, STRIPS - 1, moving, 0, unroll=MOVE)

    def window_loop(i, carry):
        base = OFF + 8 * i
        rows = aligned(base)
        pull = [0.0, 0.0]
        for b in range(BANDS):
            here = wv[b, :, rows, :]
            fields = (
                wv[b, 0:2, pl.ds(base + 1, 8), :] - wv[b, 0:2, pl.ds(base - 1, 8), :],
                across(here)[:2],
                SIGMA * (here[:2] - f1v[b, :, rows, :]),
            )
            pull = store_data(fields, b, slice(0, 2), rows, pull)
        for c in range(2):
            p1[c, 0:2, rows, :] = pull[c]
        return carry

    lax.fori_loop(1, T // 8 - 1, window_loop, 0, unroll=5)

    def edge(base, right, left):
        rows = aligned(base)

        def pick(x, y):
            return jnp.where(right_side, pltpu.roll(x, back(right[1]), 1), pltpu.roll(y, back(left[1]), 1))

        def near(shift, step):
            return own[pl.ds(base + shift[0] + step, 8), :]

        here = pick(near(right, 0), near(left, 0))
        down = pick(near(right, 1) - near(right, -1), near(left, 1) - near(left, -1))
        x = eq[rows, :]
        first = jnp.where(right_side, roll(x, 6, 1), roll(x, -4, 1))
        kinds = []
        for field in (down, next_minus_prev(here, 1), SIGMA * (here - first)):
            kinds.append(jnp.where((place >= 6) & (place < 10), field, roll(field, 60, 1)))
        pull = [0.0, 0.0]
        for b in range(BANDS):
            fields = [roll(kind, -(16 * b + 6), 1) for kind in kinds]
            pull = store_data(fields, b, 2, rows, pull)
        for c in range(2):
            p1[c, 2, rows, :] = pull[c]

    side_shifts = shift_at((0, 1)), shift_at((0, -1))

    def edge_loop(i, carry):
        edge(OFF + 8 * i, *side_shifts)
        return carry

    lax.fori_loop(1, T // 8 - 1, edge_loop, 0, unroll=EDGE)

    for copy, diagonal in sends[:raw_count]:
        if diagonal:
            copy.wait()
    keep_above = jnp.where(me_r == 0, 0.0, 1.0) * keep_lane
    keep_below = jnp.where(me_r == n_r - 1, 0.0, 1.0) * keep_lane
    side16 = lax.broadcasted_iota(jnp.int32, (16, 128), 1) < 64
    eq[OFF - 16:OFF, :] = jnp.where(side16, kr[at((-1, 1))], kr[at((-1, -1))]) * keep_above
    eq[OFF + T:OFF + T + 16, :] = jnp.where(side16, kr[at((1, 1))], kr[at((1, -1))]) * keep_below
    for i in (0, 1, STRIPS, STRIPS + 1):
        third(i, 0)

    def outermost(j, carry):
        moving(j * (STRIPS - 1), 0)
        moving(j * (STRIPS - 3) + 1, 0)
        return carry

    lax.fori_loop(0, 2, outermost, 0, unroll=2)
    lax.fori_loop(0, 2, lambda j, carry: window_loop(j * (T // 8 - 1), carry), 0, unroll=2)
    window(OFF - 8, shift_at((-1, 0)))
    window(OFF + T, shift_at((1, 0)))
    lax.fori_loop(0, 2, lambda j, carry: edge_loop(j * (T // 8 - 1), carry), 0, unroll=2)
    edge(OFF - 8, shift_at((-1, 1)), shift_at((-1, -1)))
    edge(OFF + T, shift_at((1, 1)), shift_at((1, -1)))

    crow = lax.broadcasted_iota(jnp.int32, (CROWS, 128), 0) - 8 + me_r * CT
    clane = lax.broadcasted_iota(jnp.int32, (CROWS, 128), 1)
    ccol = jnp.where(clane < 64, clane, clane - 128) + me_c * CT
    mask = jnp.where((crow >= 0) & (crow < n_r * CT) & (ccol >= 0) & (ccol < n_c * CT), 1.0, 0.0)
    for copy, _ in sends[raw_count:]:
        copy.wait()
    means = []
    for frame in range(2):
        def column(dc):
            parts = [cr[at((-1, dc)), frame]]
            turn = CT * dc
            if dc == 0:
                parts.append(ce[frame, 8:8 + CT, :])
            else:
                for half in range(2):
                    n = 2 * frame + half
                    side = cr[at((0, dc))]
                    side = jnp.concatenate([side[0], side[1]], axis=0)
                    parts.append(roll(side, (0 if dc > 0 else 24) - 8 * n, 1))
            parts.append(cr[at((1, dc)), frame])
            return roll(jnp.concatenate(parts, axis=0), turn, 1)

        mine, right, left = column(0), column(1), column(-1)
        bands = []
        for b in range(BANDS):
            mix = jnp.where(clane // CT == (b + 1) % 4, right, jnp.where(clane // CT == (b + 3) % 4, left, mine))
            bands.append(roll(mix, -CT * b, 1) * mask)
        means.append(bands)
    grad_r = [0.5 * next_minus_prev(x, 0) for x in means[1]]
    grad_c = [0.5 * next_minus_prev(x, 1) for x in means[1]]
    off = [means[1][b] - means[0][b] for b in range(BANDS)]
    now = [jnp.zeros((CROWS, 128), F32)] * 2
    bar = now
    dual_r, dual_c = list(now), list(now)
    data = [jnp.zeros((CROWS, 128), F32)] * BANDS
    for it in range(3):
        div = [0.0, 0.0]
        if it > 0:
            for c in range(2):
                pr = dual_r[c] + (0.5 * SIGMA) * next_minus_prev(bar[c], 0)
                pc = dual_c[c] + (0.5 * SIGMA) * next_minus_prev(bar[c], 1)
                k = shrink(pr * pr + pc * pc) * mask
                dual_r[c], dual_c[c] = pr * k, pc * k
                div[c] = 0.5 * (next_minus_prev(dual_r[c], 0) + next_minus_prev(dual_c[c], 1))
        pull = [0.0, 0.0]
        for b in range(BANDS):
            rho = off[b]
            if it > 0:
                rho = rho + grad_r[b] * bar[0] + grad_c[b] * bar[1]
            data[b] = jnp.clip(data[b] + SIGMA * rho, -LAM, LAM)
            pull = [pull[0] + data[b] * grad_r[b], pull[1] + data[b] * grad_c[b]]
        later = [(now[c] + TAU * (div[c] - pull[c])) * mask for c in range(2)]
        bar = [2.0 * later[c] - now[c] for c in range(2)]
        now = later
    for c in range(2):
        coarse_ref[c] = now[c][8:8 + CT, 0:CT]

    wide_shape = (128, 128 * PANELS)
    wide = lax.broadcasted_iota(jnp.int32, wide_shape, 1)
    source = jnp.where(wide < T + 64, wide // FACTOR, 128 - (128 * PANELS - wide + FACTOR - 1) // FACTOR)
    spread = jnp.where(lax.broadcasted_iota(jnp.int32, wide_shape, 0) == source, 1.0, 0.0).astype(BF16)
    block_lane = lax.broadcasted_iota(jnp.int32, (PANELS, CROWS, 128), 2)
    block_lane = block_lane + 128 * lax.broadcasted_iota(jnp.int32, (PANELS, CROWS, 128), 0)
    block_row = lax.broadcasted_iota(jnp.int32, (PANELS, CROWS, 128), 1) - 8 + me_r * CT
    block_col = jnp.where(block_lane < T + 64, block_lane, block_lane - 128 * PANELS) + me_c * T
    block_mask = jnp.where(
        (block_row >= 0) & (block_row < n_r * CT) & (block_col >= 0) & (block_col < n_c * T), 1.0, 0.0
    )
    for c in range(2):
        repeated = dot_split(now[c], spread, 3)
        t = jnp.stack([repeated[:, 128 * k:128 * k + 128] for k in range(PANELS)])
        first_r = t - roll(t, 1, 1)
        last_r = roll(t, -1, 1) - t
        step_c = across(t)
        square = step_c * step_c
        k_first = shrink(first_r * first_r + square) * block_mask
        k_inner = shrink(square) * block_mask
        k_last = shrink(last_r * last_r + square) * block_mask
        pr_first, pr_last = first_r * k_first, last_r * k_last
        pc_first, pc_inner, pc_last = step_c * k_first, step_c * k_inner, step_c * k_last
        inner = across(pc_inner)
        for n, value in enumerate((
            t, pr_first, pr_last, pc_first, pc_inner, pc_last,
            across(pc_first) - roll(pr_last, 1, 1), inner - pr_first, inner, inner + pr_last,
            across(pc_last) + roll(pr_first, -1, 1),
        )):
            tc[n, c] = value

    def block_row_of(n, c, s):
        return jnp.broadcast_to(tc[n, c, :, pl.ds(s + 7, 1), :], (PANELS, 8, 128))

    panel_sub = lax.broadcasted_iota(jnp.int32, (PANELS, 8, 128), 1)
    right_in = jnp.where(me_c == n_c - 1, 0.0, 1.0)
    left_in = jnp.where(me_c == 0, 0.0, 1.0)
    col_mask = jnp.where(panel_lane[:1] < 64, right_in, left_in)

    def inside_cols(x):
        return jnp.concatenate([x[:2], x[2:] * col_mask], axis=0)

    def clear_rows(ref):
        @pl.when(me_r == 0)
        def _():
            ref[:, :, FIRST:FIRST + 8, :] = jnp.zeros((2, PANELS, 8, 128), F32)

        @pl.when(me_r == n_r - 1)
        def _():
            ref[:, :, OFF + T:OFF + T + 8, :] = jnp.zeros((2, PANELS, 8, 128), F32)

    def opening(s, carry):
        rows = aligned(FIRST + 8 * s)
        for c in range(2):
            t, pr_first, pr_last, pc_first, pc_inner, pc_last, d0, d1, dm, d6, d7 = [
                block_row_of(n, c, s) for n in range(11)
            ]
            at0, at7 = panel_sub == 0, panel_sub == 7
            div = jnp.where(at0, d0, jnp.where(at7, d7, jnp.where(panel_sub == 1, d1, jnp.where(panel_sub == 6, d6, dm))))
            prv[c, :, rows, :] = jnp.where(at0, pr_first, jnp.where(at7, pr_last, 0.0))
            pcv[c, :, rows, :] = jnp.where(at0, pc_first, jnp.where(at7, pc_last, pc_inner))
            later = t + (1.0 / 64.0) * (div - p1[c, :, rows, :])
            u[c, :, rows, :] = later
            ub[c, :, rows, :] = inside_cols(2.0 * later - t)
        return carry

    lax.fori_loop(0, STRIPS, opening, 0, unroll=UNROLL)
    clear_rows(ub)

    for it in (1, 2):
        def dual(s, carry):
            base = FIRST + 8 * s
            rows = aligned(base)
            for c in range(2):
                pr = prv[c, :, rows, :] + (ub[c, :, pl.ds(base + 1, 8), :] - ub[c, :, pl.ds(base - 1, 8), :])
                pc = pcv[c, :, rows, :] + across(ub[c, :, rows, :])
                k = inside_cols(shrink(pr * pr + pc * pc))
                prv[c, :, rows, :] = pr * k
                pcv[c, :, rows, :] = pc * k
            return carry

        lax.fori_loop(0, STRIPS, dual, 0, unroll=UNROLL)
        clear_rows(prv)

        def primal(s, carry):
            base = FIRST + 8 * s
            rows = aligned(base)
            n = PANELS if it < 2 else 2
            step = [(ub[c, :, rows, :] - block_row_of(0, c, s))[:n] for c in range(2)]
            pull = [0.0, 0.0]
            for b in range(BANDS):
                gr, gc = g[b, 0:n, rows, :], g[BANDS + b, 0:n, rows, :]
                value = a[b, 0:n, rows, :] + gr * step[0] + gc * step[1]
                if it == 2:
                    value = value + g[2 * BANDS + b, 0:n, rows, :]
                value = jnp.clip(value, -LAM, LAM)
                if it < 2:
                    a[b, :, rows, :] = value
                pull = [pull[0] + value * gr, pull[1] + value * gc]
            for c in range(2):
                div = (
                    prv[c, 0:n, pl.ds(base + 1, 8), :] - prv[c, 0:n, pl.ds(base - 1, 8), :]
                    + across(pcv[c, :, rows, :])[:n]
                )
                was = u[c, 0:n, rows, :]
                later = was + (1.0 / 64.0) * (div - pull[c])
                if it < 2:
                    u[c, :, rows, :] = later
                    ub[c, :, rows, :] = inside_cols(2.0 * later - was)
                else:
                    for k in range(2):
                        flow_ref[c, aligned(base - OFF), 128 * k:128 * k + 128] = 8.0 * later[k]
            return carry

        if it < 2:
            lax.fori_loop(0, STRIPS, primal, 0, unroll=UNROLL)
            clear_rows(ub)
        else:
            lax.fori_loop(1, STRIPS - 1, primal, 0, unroll=8)


def local(frame_first, frame_second, shifts):
    vmem = pltpu.VMEM
    field = vmem((2, PANELS, ROWS, 128), F32)
    return pl.pallas_call(
        kernel,
        out_shape=(
            vmem((2, T, T), F32),
            vmem((2, CT, CT), F32),
        ),
        in_specs=[
            pl.BlockSpec(memory_space=pl.ANY),
            pl.BlockSpec(memory_space=pl.ANY),
            pl.BlockSpec(memory_space=pltpu.SMEM),
        ],
        out_specs=(pl.BlockSpec(memory_space=vmem), pl.BlockSpec(memory_space=vmem)),
        scratch_shapes=[
            vmem((BANDS, PANELS, ROWS, 128), F32),
            vmem((BANDS, PANELS, ROWS, 128), F32),
            vmem((BANDS, 2, ROWS, 128), F32),
            vmem((3 * BANDS, PANELS, ROWS, 128), F32),
            vmem((BANDS, PANELS, ROWS, 128), F32),
            field, field, field, field, field,
            vmem((11, 2, PANELS, CROWS, 128), F32),
            vmem((2, CROWS, 128), F32),
            vmem((2, 2, 8, 128), F32),
            vmem((8, 2, 8, 128), F32),
            vmem((T, 128), F32),
            vmem((2, T // 2, 128), F32),
            vmem((2, T // 2, 128), F32),
            vmem((8, 16, 128), F32),
            vmem((ROWS, 128), F32),
            vmem((ROWS, 128), F32),
            vmem((8, 128), jnp.int32),
            vmem((8, 8, 128), jnp.int32),
            pltpu.SemaphoreType.DMA((4,)),
            pltpu.SemaphoreType.DMA((32,)),
            pltpu.SemaphoreType.DMA((32,)),
        ],
        compiler_params=pltpu.CompilerParams(
            collective_id=0, has_side_effects=True, vmem_limit_bytes=60 * 1024 * 1024
        ),
    )(frame_first, frame_second, shifts)


def solution(mesh):
    return jax.shard_map(
        local,
        mesh=mesh,
        in_specs=(P(None, "row", "col"), P(None, "row", "col"), P("row", "col", None)),
        out_specs=(P(None, "row", "col"), P(None, "row", "col")),
        check_vma=False,
    )
```

```python
import jax
import jax.numpy as jnp
from jax import lax
from jax.experimental import pallas as pl
from jax.experimental.pallas import tpu as pltpu
from jax.sharding import PartitionSpec as P

FACTOR = 8
TAU = 0.25
SIGMA = 0.25
LAM = 0.3
ALPHA = 0.3
BANDS = 4
T = 256
CT = T // FACTOR
OFF = 24
ROWS = T + 2 * OFF
FIRST = OFF - 8
STRIPS = T // 8 + 2
UNROLL = STRIPS // 2
MOVE = 16
EDGE = 10
PANELS = 3
DEEP = 9
THIN = 4
CROWS = CT + 16
F32 = jnp.float32
BF16 = jnp.bfloat16
DIRECTIONS = [(-1, -1), (-1, 1), (1, -1), (1, 1), (0, -1), (0, 1), (-1, 0), (1, 0)]


def split3(x):
    hi = x.astype(BF16)
    rest = x - hi.astype(F32)
    mid = rest.astype(BF16)
    low = (rest - mid.astype(F32)).astype(BF16)
    return hi, mid, low


def dot_split(x, w, parts):
    total = None
    for piece in split3(x)[:parts]:
        term = jnp.dot(piece, w, preferred_element_type=F32)
        total = term if total is None else total + term
    return total


def roll(x, amount, axis):
    amount = amount % x.shape[axis]
    return x if amount == 0 else pltpu.roll(x, amount, axis)


def next_minus_prev(x, axis):
    return roll(x, -1, axis) - roll(x, 1, axis)


def following(x):
    return jnp.concatenate([x[1:], x[:1]], axis=0)


def preceding(x):
    return jnp.concatenate([x[-1:], x[:-1]], axis=0)


def across(x):
    lane = lax.broadcasted_iota(jnp.int32, x.shape, 2)
    ahead, behind = roll(x, -1, 2), roll(x, 1, 2)
    return jnp.where(lane == 127, following(ahead), ahead) - jnp.where(lane == 0, preceding(behind), behind)


def shrink(square):
    return jnp.minimum(1.0, ALPHA * lax.rsqrt(square))


def aligned(start, size=8):
    return pl.ds(pl.multiple_of(start, 8), size)


def kernel(
    f1_ref, f2_ref, sh_ref, flow_ref, coarse_ref,
    s2, wv, f1v, g, a, p1, u, ub, prv, pcv, tc, ce, cs, cr,
    pack, es, er, kr, eq, own, shs, shr,
    local_sem, send_sem, recv_sem,
):
    me_r, me_c = lax.axis_index("row"), lax.axis_index("col")
    n_r, n_c = lax.axis_size("row"), lax.axis_size("col")

    def device(direction):
        dr, dc = direction
        return (lax.rem(me_r + dr + n_r, n_r), lax.rem(me_c + dc + n_c, n_c))

    def exists(direction):
        row, col = me_r + direction[0], me_c + direction[1]
        return (row >= 0) & (row < n_r) & (col >= 0) & (col < n_c)

    present = {d: exists(d) for d in DIRECTIONS}
    barrier = pltpu.get_barrier_semaphore()
    for direction in DIRECTIONS:
        @pl.when(present[direction])
        def _():
            pl.semaphore_signal(barrier, inc=1, device_id=device(direction), device_id_type=pl.DeviceIdType.MESH)
    gets = []
    for ref, kept in ((f2_ref, s2), (f1_ref, f1v)):
        for k in range(2):
            copy = pltpu.make_async_copy(
                ref.at[:, :, pl.ds(128 * k, 128)], kept.at[:, k, pl.ds(OFF, T), :], local_sem.at[len(gets)]
            )
            copy.start()
            gets.append(copy)
    my_shift = (sh_ref[0, 0, 0], sh_ref[0, 0, 1])
    sub8 = lax.broadcasted_iota(jnp.int32, (8, 128), 0)
    shs[...] = jnp.where(sub8 == 0, my_shift[0], my_shift[1])

    for direction in DIRECTIONS:
        @pl.when(jnp.logical_not(present[direction]))
        def _():
            n = DIRECTIONS.index(direction)
            shr[n] = jnp.zeros((8, 128), jnp.int32)
            cr[n] = jnp.zeros((2, 8, 128), F32)
            kr[n] = jnp.zeros((16, 128), F32)
            if direction[0] == 0:
                er[0 if direction[1] > 0 else 1] = jnp.zeros((T // 2, 128), F32)
            if direction[1] == 0:
                base = OFF - 8 if direction[0] < 0 else OFF + T
                f1v[:, :, base:base + 8, :] = jnp.zeros((BANDS, 2, 8, 128), F32)

    sends = []

    def send(src, dst, direction):
        slot = len(sends)
        copy = pltpu.make_async_remote_copy(
            src_ref=src, dst_ref=dst, send_sem=send_sem.at[slot], recv_sem=recv_sem.at[slot],
            device_id=device(direction), device_id_type=pl.DeviceIdType.MESH,
        )
        sends.append((copy, direction))

    def start(copies):
        for direction in DIRECTIONS:
            @pl.when(present[direction])
            def _():
                for copy, way in copies:
                    if way == direction:
                        copy.start()

    def finish(copies):
        for direction in DIRECTIONS:
            ours = [copy for copy, way in copies if way == direction]
            if ours:
                @pl.when(present[direction])
                def _():
                    for copy in ours:
                        copy.wait_send()

                @pl.when(present[-direction[0], -direction[1]])
                def _():
                    for copy in ours:
                        copy.wait_recv()

    lane = lax.broadcasted_iota(jnp.int32, (8, 128), 1)
    place = lane % 16
    right_side = lane < 64
    tall = lax.broadcasted_iota(jnp.int32, (T // 2, 128), 1) < 64
    for copy in gets:
        copy.wait()

    def packing(i, carry):
        rows = aligned(OFF + 8 * i)
        acc = jnp.zeros((8, 128), F32)
        for b in range(BANDS):
            left2, right2, left1, right1 = s2[b, 0, rows, :], s2[b, 1, rows, :], f1v[b, 0, rows, :], f1v[b, 1, rows, :]
            left = jnp.where(place < 6, roll(left1, 16 * b, 1), roll(left2, 16 * b + 6, 1))
            right = jnp.where(place < 10, roll(right2, 16 * b + 74, 1), roll(right1, 16 * b + 78, 1))
            acc = jnp.where(lane // 16 == b, left, jnp.where(lane // 16 == b + 4, right, acc))
        pack[aligned(8 * i), :] = acc
        return carry

    lax.fori_loop(0, T // 8, packing, 0, unroll=32)
    upper, lower = pack[0:128, :], pack[128:256, :]
    es[0] = jnp.where(tall, upper, roll(lower, 64, 1))
    es[1] = jnp.where(tall, roll(upper, 64, 1), lower)

    pl.semaphore_wait(barrier, sum(here.astype(jnp.int32) for here in present.values()))

    for dr, dc in DIRECTIONS:
        seen = DIRECTIONS.index((-dr, -dc))
        if dr != 0 and dc != 0:
            send(pack.at[pl.ds(0 if dr < 0 else T - 16, 16), :], kr.at[seen], (dr, dc))
        elif dr == 0:
            side = 0 if dc < 0 else 1
            send(es.at[side], er.at[side], (dr, dc))
        else:
            from2, to2 = (OFF, OFF + T) if dr < 0 else (OFF + T - DEEP, OFF - DEEP)
            from1, to1 = (OFF, OFF + T) if dr < 0 else (OFF + T - THIN, OFF - THIN)
            both = pl.ds(0, 2)
            send(s2.at[:, both, pl.ds(from2, DEEP), :], s2.at[:, both, pl.ds(to2, DEEP), :], (dr, dc))
            send(f1v.at[:, both, pl.ds(from1, THIN), :], f1v.at[:, both, pl.ds(to1, THIN), :], (dr, dc))
        send(shs, shr.at[seen], (dr, dc))
    raw_sends = list(sends)
    start(raw_sends)

    col_id = lax.broadcasted_iota(jnp.int32, (128, 128), 0) // FACTOR
    lane_id = lax.broadcasted_iota(jnp.int32, (128, 128), 1)
    row_sum = (
        lax.broadcasted_iota(jnp.int32, (CT, T), 1) // FACTOR == lax.broadcasted_iota(jnp.int32, (CT, T), 0)
    ).astype(F32).astype(BF16)
    for frame in range(2):
        total = jnp.zeros((T, 128), F32)
        for b in range(BANDS):
            for k in range(2):
                block = (f1v if frame == 0 else s2)[b, k, OFF:OFF + T, :]
                weights = jnp.where(lane_id - CT * b - 16 * k == col_id, 1.0 / 64.0, 0.0).astype(BF16)
                total = total + dot_split(block, weights, 2)
        hi, mid, _ = split3(total)
        ce[frame, 8:8 + CT, :] = (
            jnp.dot(row_sum, hi, preferred_element_type=F32) + jnp.dot(row_sum, mid, preferred_element_type=F32)
        )
    group = (lax.broadcasted_iota(jnp.int32, (16, 128), 1) % CT) // 8
    edge_l = edge_r = jnp.zeros((16, 128), F32)
    for frame in range(2):
        for half in range(2):
            n = 2 * frame + half
            piece = ce[frame, 8 + 16 * half:24 + 16 * half, :]
            edge_l = jnp.where(group == n, roll(piece, 8 * n, 1), edge_l)
            edge_r = jnp.where(group == n, roll(piece, 8 * n - 24, 1), edge_r)
    for half in range(2):
        cs[0, half] = edge_l[8 * half:8 * half + 8]
        cs[1, half] = edge_r[8 * half:8 * half + 8]

    for dr, dc in DIRECTIONS:
        seen = DIRECTIONS.index((-dr, -dc))
        if dr == 0:
            send(cs.at[0 if dc < 0 else 1], cr.at[seen], (dr, dc))
        else:
            send(ce.at[:, pl.ds(8 if dr < 0 else CT, 8), :], cr.at[seen], (dr, dc))
    coarse_sends = sends[len(raw_sends):]
    start(coarse_sends)

    def own_edge(start):
        acc = jnp.zeros((8, 128), F32)
        for b in range(BANDS):
            left, right = s2[b, 0, aligned(start), :], s2[b, 1, aligned(start), :]
            acc = jnp.where(lane // 16 == b, roll(right, 16 * b + 6, 1), acc)
            acc = jnp.where(lane // 16 == b + 4, roll(left, 16 * b + 74, 1), acc)
        return acc

    def owning(i, carry):
        own[aligned(OFF + 8 * i), :] = own_edge(OFF + 8 * i)
        return carry

    lax.fori_loop(0, T // 8, owning, 0, unroll=8)

    finish([(copy, way) for copy, way in raw_sends if 0 in way])

    def at(direction):
        return DIRECTIONS.index(direction)

    def shift_at(d):
        return shr[at(d), 0, 0], shr[at(d), 1, 0]

    keep_lane = jnp.where(
        lane[0:1] < 64, jnp.where(me_c == n_c - 1, 0.0, 1.0), jnp.where(me_c == 0, 0.0, 1.0)
    )
    eq[OFF:OFF + 128, :] = jnp.where(tall, er[0], roll(er[1], 64, 1)) * keep_lane
    eq[OFF + 128:OFF + 256, :] = jnp.where(tall, roll(er[0], 64, 1), er[1]) * keep_lane

    @pl.when(me_r == 0)
    def _():
        s2[:, 0:2, OFF - 16:OFF, :] = jnp.zeros((BANDS, 2, 16, 128), F32)

    @pl.when(me_r == n_r - 1)
    def _():
        s2[:, 0:2, OFF + T:OFF + T + 16, :] = jnp.zeros((BANDS, 2, 16, 128), F32)

    for start in (OFF - 16, OFF - 8, OFF + T, OFF + T + 8):
        own[start:start + 8, :] = own_edge(start)

    theirs = (right_side & (place >= 6)) | ((lane >= 64) & (place < 10))

    def third(i, carry):
        rows = aligned(OFF - 16 + 8 * i)
        x = eq[rows, :]
        mix = jnp.where((place >= 6) & (place < 13), x, roll(x, 60, 1))
        for b in range(BANDS):
            s2[b, 2, rows, :] = roll(mix, -(16 * b + 6), 1)
        own[rows, :] = jnp.where(theirs, x, own[rows, :])
        return carry

    lax.fori_loop(2, STRIPS, third, 0, unroll=16)

    panel_lane = lax.broadcasted_iota(jnp.int32, (PANELS, 8, 128), 2)

    def back(shift):
        return jnp.where(shift > 0, 128 - shift, -shift)

    def store_data(fields, b, panels, rows, pull):
        dr, dc, wf = fields
        first = jnp.clip(wf, -LAM, LAM)
        g[b, panels, rows, :] = dr
        g[BANDS + b, panels, rows, :] = dc
        g[2 * BANDS + b, panels, rows, :] = wf
        a[b, panels, rows, :] = first + wf
        return [pull[0] + first * dr, pull[1] + first * dc]

    def window(base, shift):
        rows = aligned(base)
        start = base + shift[0]
        amount = back(shift[1])
        over = panel_lane + shift[1] >= 128
        under = panel_lane + shift[1] < 0

        def shifted(x):
            turned = pltpu.roll(x, amount, 2)
            return jnp.where(over, following(turned), jnp.where(under, preceding(turned), turned))

        pull = [0.0, 0.0]
        for b in range(BANDS):
            here = shifted(s2[b, :, pl.ds(start, 8), :])
            down = shifted(s2[b, :, pl.ds(start + 1, 8), :] - s2[b, :, pl.ds(start - 1, 8), :])
            fields = (down[:2], across(here)[:2], SIGMA * (here[:2] - f1v[b, :, rows, :]))
            pull = store_data(fields, b, slice(0, 2), rows, pull)
        for c in range(2):
            p1[c, 0:2, rows, :] = pull[c]

    amount = back(my_shift[1])
    over = panel_lane + my_shift[1] >= 128
    under = panel_lane + my_shift[1] < 0

    def moving(s, carry):
        base = FIRST + 8 * s
        for b in range(BANDS):
            turned = pltpu.roll(s2[b, :, pl.ds(base + my_shift[0], 8), :], amount, 2)
            wv[b, :, aligned(base), :] = jnp.where(
                over, following(turned), jnp.where(under, preceding(turned), turned)
            )
        return carry

    lax.fori_loop(1, STRIPS - 1, moving, 0, unroll=MOVE)

    def window_loop(i, carry):
        base = OFF + 8 * i
        rows = aligned(base)
        pull = [0.0, 0.0]
        for b in range(BANDS):
            here = wv[b, :, rows, :]
            fields = (
                wv[b, 0:2, pl.ds(base + 1, 8), :] - wv[b, 0:2, pl.ds(base - 1, 8), :],
                across(here)[:2],
                SIGMA * (here[:2] - f1v[b, :, rows, :]),
            )
            pull = store_data(fields, b, slice(0, 2), rows, pull)
        for c in range(2):
            p1[c, 0:2, rows, :] = pull[c]
        return carry

    lax.fori_loop(1, T // 8 - 1, window_loop, 0, unroll=5)

    def edge(base, right, left):
        rows = aligned(base)

        def pick(x, y):
            return jnp.where(right_side, pltpu.roll(x, back(right[1]), 1), pltpu.roll(y, back(left[1]), 1))

        def near(shift, step):
            return own[pl.ds(base + shift[0] + step, 8), :]

        here = pick(near(right, 0), near(left, 0))
        down = pick(near(right, 1) - near(right, -1), near(left, 1) - near(left, -1))
        x = eq[rows, :]
        first = jnp.where(right_side, roll(x, 6, 1), roll(x, -4, 1))
        kinds = []
        for field in (down, next_minus_prev(here, 1), SIGMA * (here - first)):
            kinds.append(jnp.where((place >= 6) & (place < 10), field, roll(field, 60, 1)))
        pull = [0.0, 0.0]
        for b in range(BANDS):
            fields = [roll(kind, -(16 * b + 6), 1) for kind in kinds]
            pull = store_data(fields, b, 2, rows, pull)
        for c in range(2):
            p1[c, 2, rows, :] = pull[c]

    side_shifts = shift_at((0, 1)), shift_at((0, -1))

    def edge_loop(i, carry):
        edge(OFF + 8 * i, *side_shifts)
        return carry

    lax.fori_loop(1, T // 8 - 1, edge_loop, 0, unroll=EDGE)

    finish([(copy, way) for copy, way in raw_sends if 0 not in way])
    keep_above = jnp.where(me_r == 0, 0.0, 1.0) * keep_lane
    keep_below = jnp.where(me_r == n_r - 1, 0.0, 1.0) * keep_lane
    side16 = lax.broadcasted_iota(jnp.int32, (16, 128), 1) < 64
    eq[OFF - 16:OFF, :] = jnp.where(side16, kr[at((-1, 1))], kr[at((-1, -1))]) * keep_above
    eq[OFF + T:OFF + T + 16, :] = jnp.where(side16, kr[at((1, 1))], kr[at((1, -1))]) * keep_below
    for i in (0, 1, STRIPS, STRIPS + 1):
        third(i, 0)

    def outermost(j, carry):
        moving(j * (STRIPS - 1), 0)
        moving(j * (STRIPS - 3) + 1, 0)
        return carry

    lax.fori_loop(0, 2, outermost, 0, unroll=2)
    lax.fori_loop(0, 2, lambda j, carry: window_loop(j * (T // 8 - 1), carry), 0, unroll=2)
    window(OFF - 8, shift_at((-1, 0)))
    window(OFF + T, shift_at((1, 0)))
    lax.fori_loop(0, 2, lambda j, carry: edge_loop(j * (T // 8 - 1), carry), 0, unroll=2)
    edge(OFF - 8, shift_at((-1, 1)), shift_at((-1, -1)))
    edge(OFF + T, shift_at((1, 1)), shift_at((1, -1)))

    crow = lax.broadcasted_iota(jnp.int32, (CROWS, 128), 0) - 8 + me_r * CT
    clane = lax.broadcasted_iota(jnp.int32, (CROWS, 128), 1)
    ccol = jnp.where(clane < 64, clane, clane - 128) + me_c * CT
    mask = jnp.where((crow >= 0) & (crow < n_r * CT) & (ccol >= 0) & (ccol < n_c * CT), 1.0, 0.0)
    finish(coarse_sends)
    means = []
    for frame in range(2):
        def column(dc):
            parts = [cr[at((-1, dc)), frame]]
            turn = CT * dc
            if dc == 0:
                parts.append(ce[frame, 8:8 + CT, :])
            else:
                for half in range(2):
                    n = 2 * frame + half
                    side = cr[at((0, dc))]
                    side = jnp.concatenate([side[0], side[1]], axis=0)
                    parts.append(roll(side, (0 if dc > 0 else 24) - 8 * n, 1))
            parts.append(cr[at((1, dc)), frame])
            return roll(jnp.concatenate(parts, axis=0), turn, 1)

        mine, right, left = column(0), column(1), column(-1)
        bands = []
        for b in range(BANDS):
            mix = jnp.where(clane // CT == (b + 1) % 4, right, jnp.where(clane // CT == (b + 3) % 4, left, mine))
            bands.append(roll(mix, -CT * b, 1) * mask)
        means.append(bands)
    grad_r = [0.5 * next_minus_prev(x, 0) for x in means[1]]
    grad_c = [0.5 * next_minus_prev(x, 1) for x in means[1]]
    off = [means[1][b] - means[0][b] for b in range(BANDS)]
    now = [jnp.zeros((CROWS, 128), F32)] * 2
    bar = now
    dual_r, dual_c = list(now), list(now)
    data = [jnp.zeros((CROWS, 128), F32)] * BANDS
    for it in range(3):
        div = [0.0, 0.0]
        if it > 0:
            for c in range(2):
                pr = dual_r[c] + (0.5 * SIGMA) * next_minus_prev(bar[c], 0)
                pc = dual_c[c] + (0.5 * SIGMA) * next_minus_prev(bar[c], 1)
                k = shrink(pr * pr + pc * pc) * mask
                dual_r[c], dual_c[c] = pr * k, pc * k
                div[c] = 0.5 * (next_minus_prev(dual_r[c], 0) + next_minus_prev(dual_c[c], 1))
        pull = [0.0, 0.0]
        for b in range(BANDS):
            rho = off[b]
            if it > 0:
                rho = rho + grad_r[b] * bar[0] + grad_c[b] * bar[1]
            data[b] = jnp.clip(data[b] + SIGMA * rho, -LAM, LAM)
            pull = [pull[0] + data[b] * grad_r[b], pull[1] + data[b] * grad_c[b]]
        later = [(now[c] + TAU * (div[c] - pull[c])) * mask for c in range(2)]
        bar = [2.0 * later[c] - now[c] for c in range(2)]
        now = later
    for c in range(2):
        coarse_ref[c] = now[c][8:8 + CT, 0:CT]

    wide_shape = (128, 128 * PANELS)
    wide = lax.broadcasted_iota(jnp.int32, wide_shape, 1)
    source = jnp.where(wide < T + 64, wide // FACTOR, 128 - (128 * PANELS - wide + FACTOR - 1) // FACTOR)
    spread = jnp.where(lax.broadcasted_iota(jnp.int32, wide_shape, 0) == source, 1.0, 0.0).astype(BF16)
    block_lane = lax.broadcasted_iota(jnp.int32, (PANELS, CROWS, 128), 2)
    block_lane = block_lane + 128 * lax.broadcasted_iota(jnp.int32, (PANELS, CROWS, 128), 0)
    block_row = lax.broadcasted_iota(jnp.int32, (PANELS, CROWS, 128), 1) - 8 + me_r * CT
    block_col = jnp.where(block_lane < T + 64, block_lane, block_lane - 128 * PANELS) + me_c * T
    block_mask = jnp.where(
        (block_row >= 0) & (block_row < n_r * CT) & (block_col >= 0) & (block_col < n_c * T), 1.0, 0.0
    )
    for c in range(2):
        repeated = dot_split(now[c], spread, 3)
        t = jnp.stack([repeated[:, 128 * k:128 * k + 128] for k in range(PANELS)])
        first_r = t - roll(t, 1, 1)
        last_r = roll(t, -1, 1) - t
        step_c = across(t)
        square = step_c * step_c
        k_first = shrink(first_r * first_r + square) * block_mask
        k_inner = shrink(square) * block_mask
        k_last = shrink(last_r * last_r + square) * block_mask
        pr_first, pr_last = first_r * k_first, last_r * k_last
        pc_first, pc_inner, pc_last = step_c * k_first, step_c * k_inner, step_c * k_last
        inner = across(pc_inner)
        for n, value in enumerate((
            t, pr_first, pr_last, pc_first, pc_inner, pc_last,
            across(pc_first) - roll(pr_last, 1, 1), inner - pr_first, inner, inner + pr_last,
            across(pc_last) + roll(pr_first, -1, 1),
        )):
            tc[n, c] = value

    def block_row_of(n, c, s):
        return jnp.broadcast_to(tc[n, c, :, pl.ds(s + 7, 1), :], (PANELS, 8, 128))

    panel_sub = lax.broadcasted_iota(jnp.int32, (PANELS, 8, 128), 1)
    right_in = jnp.where(me_c == n_c - 1, 0.0, 1.0)
    left_in = jnp.where(me_c == 0, 0.0, 1.0)
    col_mask = jnp.where(panel_lane[:1] < 64, right_in, left_in)

    def inside_cols(x):
        return jnp.concatenate([x[:2], x[2:] * col_mask], axis=0)

    def clear_rows(ref):
        @pl.when(me_r == 0)
        def _():
            ref[:, :, FIRST:FIRST + 8, :] = jnp.zeros((2, PANELS, 8, 128), F32)

        @pl.when(me_r == n_r - 1)
        def _():
            ref[:, :, OFF + T:OFF + T + 8, :] = jnp.zeros((2, PANELS, 8, 128), F32)

    def opening(s, carry):
        rows = aligned(FIRST + 8 * s)
        for c in range(2):
            t, pr_first, pr_last, pc_first, pc_inner, pc_last, d0, d1, dm, d6, d7 = [
                block_row_of(n, c, s) for n in range(11)
            ]
            at0, at7 = panel_sub == 0, panel_sub == 7
            div = jnp.where(at0, d0, jnp.where(at7, d7, jnp.where(panel_sub == 1, d1, jnp.where(panel_sub == 6, d6, dm))))
            prv[c, :, rows, :] = jnp.where(at0, pr_first, jnp.where(at7, pr_last, 0.0))
            pcv[c, :, rows, :] = jnp.where(at0, pc_first, jnp.where(at7, pc_last, pc_inner))
            later = t + (1.0 / 64.0) * (div - p1[c, :, rows, :])
            u[c, :, rows, :] = later
            ub[c, :, rows, :] = inside_cols(2.0 * later - t)
        return carry

    lax.fori_loop(0, STRIPS, opening, 0, unroll=UNROLL)
    clear_rows(ub)

    for it in (1, 2):
        def dual(s, carry):
            base = FIRST + 8 * s
            rows = aligned(base)
            for c in range(2):
                pr = prv[c, :, rows, :] + (ub[c, :, pl.ds(base + 1, 8), :] - ub[c, :, pl.ds(base - 1, 8), :])
                pc = pcv[c, :, rows, :] + across(ub[c, :, rows, :])
                k = inside_cols(shrink(pr * pr + pc * pc))
                prv[c, :, rows, :] = pr * k
                pcv[c, :, rows, :] = pc * k
            return carry

        lax.fori_loop(0, STRIPS, dual, 0, unroll=UNROLL)
        clear_rows(prv)

        def primal(s, carry):
            base = FIRST + 8 * s
            rows = aligned(base)
            n = PANELS if it < 2 else 2
            step = [(ub[c, :, rows, :] - block_row_of(0, c, s))[:n] for c in range(2)]
            pull = [0.0, 0.0]
            for b in range(BANDS):
                gr, gc = g[b, 0:n, rows, :], g[BANDS + b, 0:n, rows, :]
                value = a[b, 0:n, rows, :] + gr * step[0] + gc * step[1]
                if it == 2:
                    value = value + g[2 * BANDS + b, 0:n, rows, :]
                value = jnp.clip(value, -LAM, LAM)
                if it < 2:
                    a[b, :, rows, :] = value
                pull = [pull[0] + value * gr, pull[1] + value * gc]
            for c in range(2):
                div = (
                    prv[c, 0:n, pl.ds(base + 1, 8), :] - prv[c, 0:n, pl.ds(base - 1, 8), :]
                    + across(pcv[c, :, rows, :])[:n]
                )
                was = u[c, 0:n, rows, :]
                later = was + (1.0 / 64.0) * (div - pull[c])
                if it < 2:
                    u[c, :, rows, :] = later
                    ub[c, :, rows, :] = inside_cols(2.0 * later - was)
                else:
                    for k in range(2):
                        flow_ref[c, aligned(base - OFF), 128 * k:128 * k + 128] = 8.0 * later[k]
            return carry

        if it < 2:
            lax.fori_loop(0, STRIPS, primal, 0, unroll=UNROLL)
            clear_rows(ub)
        else:
            lax.fori_loop(1, STRIPS - 1, primal, 0, unroll=8)


def local(frame_first, frame_second, shifts):
    vmem = pltpu.VMEM
    field = vmem((2, PANELS, ROWS, 128), F32)
    return pl.pallas_call(
        kernel,
        out_shape=(
            vmem((2, T, T), F32),
            vmem((2, CT, CT), F32),
        ),
        in_specs=[
            pl.BlockSpec(memory_space=pl.ANY),
            pl.BlockSpec(memory_space=pl.ANY),
            pl.BlockSpec(memory_space=pltpu.SMEM),
        ],
        out_specs=(pl.BlockSpec(memory_space=vmem), pl.BlockSpec(memory_space=vmem)),
        scratch_shapes=[
            vmem((BANDS, PANELS, ROWS, 128), F32),
            vmem((BANDS, PANELS, ROWS, 128), F32),
            vmem((BANDS, 2, ROWS, 128), F32),
            vmem((3 * BANDS, PANELS, ROWS, 128), F32),
            vmem((BANDS, PANELS, ROWS, 128), F32),
            field, field, field, field, field,
            vmem((11, 2, PANELS, CROWS, 128), F32),
            vmem((2, CROWS, 128), F32),
            vmem((2, 2, 8, 128), F32),
            vmem((8, 2, 8, 128), F32),
            vmem((T, 128), F32),
            vmem((2, T // 2, 128), F32),
            vmem((2, T // 2, 128), F32),
            vmem((8, 16, 128), F32),
            vmem((ROWS, 128), F32),
            vmem((ROWS, 128), F32),
            vmem((8, 128), jnp.int32),
            vmem((8, 8, 128), jnp.int32),
            pltpu.SemaphoreType.DMA((4,)),
            pltpu.SemaphoreType.DMA((32,)),
            pltpu.SemaphoreType.DMA((32,)),
        ],
        compiler_params=pltpu.CompilerParams(
            collective_id=0, has_side_effects=True, vmem_limit_bytes=60 * 1024 * 1024
        ),
    )(frame_first, frame_second, shifts)


def solution(mesh):
    return jax.shard_map(
        local,
        mesh=mesh,
        in_specs=(P(None, "row", "col"), P(None, "row", "col"), P("row", "col", None)),
        out_specs=(P(None, "row", "col"), P(None, "row", "col")),
        check_vma=False,
    )
```

```python
import jax
import jax.numpy as jnp
from jax import lax
from jax.experimental import pallas as pl
from jax.experimental.pallas import tpu as pltpu
from jax.sharding import PartitionSpec as P

FACTOR = 8
TAU = 0.25
SIGMA = 0.25
LAM = 0.3
ALPHA = 0.3
BANDS = 4
T = 256
CT = T // FACTOR
OFF = 24
ROWS = T + 2 * OFF
FIRST = OFF - 8
STRIPS = T // 8 + 2
UNROLL = STRIPS
MOVE = 16
EDGE = 10
PANELS = 3
DEEP = 9
THIN = 4
CROWS = CT + 16
F32 = jnp.float32
BF16 = jnp.bfloat16
DIRECTIONS = [(0, -1), (0, 1), (-1, -1), (-1, 1), (1, -1), (1, 1), (-1, 0), (1, 0)]


def split3(x):
    hi = x.astype(BF16)
    rest = x - hi.astype(F32)
    mid = rest.astype(BF16)
    low = (rest - mid.astype(F32)).astype(BF16)
    return hi, mid, low


def dot_split(x, w, parts):
    total = None
    for piece in split3(x)[:parts]:
        term = jnp.dot(piece, w, preferred_element_type=F32)
        total = term if total is None else total + term
    return total


def roll(x, amount, axis):
    amount = amount % x.shape[axis]
    return x if amount == 0 else pltpu.roll(x, amount, axis)


def next_minus_prev(x, axis):
    return roll(x, -1, axis) - roll(x, 1, axis)


def following(x):
    return jnp.concatenate([x[1:], x[:1]], axis=0)


def preceding(x):
    return jnp.concatenate([x[-1:], x[:-1]], axis=0)


def across(x):
    lane = lax.broadcasted_iota(jnp.int32, x.shape, 2)
    ahead, behind = roll(x, -1, 2), roll(x, 1, 2)
    return jnp.where(lane == 127, following(ahead), ahead) - jnp.where(lane == 0, preceding(behind), behind)


def shrink(square):
    return jnp.minimum(1.0, ALPHA * lax.rsqrt(square))


def aligned(start, size=8):
    return pl.ds(pl.multiple_of(start, 8), size)


def kernel(
    f1_ref, f2_ref, sh_ref, flow_ref, coarse_ref,
    s2, wv, f1v, g, a, p1, u, ub, prv, pcv, tc, ce, cs, cr,
    pack, es, er, kr, eq, own, shs, shr,
    local_sem, send_sem, recv_sem,
):
    me_r, me_c = lax.axis_index("row"), lax.axis_index("col")
    n_r, n_c = lax.axis_size("row"), lax.axis_size("col")

    def device(direction):
        dr, dc = direction
        return (lax.rem(me_r + dr + n_r, n_r), lax.rem(me_c + dc + n_c, n_c))

    def exists(direction):
        row, col = me_r + direction[0], me_c + direction[1]
        return (row >= 0) & (row < n_r) & (col >= 0) & (col < n_c)

    present = {d: exists(d) for d in DIRECTIONS}
    barrier = pltpu.get_barrier_semaphore()
    for direction in DIRECTIONS:
        @pl.when(present[direction])
        def _():
            pl.semaphore_signal(barrier, inc=1, device_id=device(direction), device_id_type=pl.DeviceIdType.MESH)
    gets = []
    for ref, kept in ((f2_ref, s2), (f1_ref, f1v)):
        for k in range(2):
            copy = pltpu.make_async_copy(
                ref.at[:, :, pl.ds(128 * k, 128)], kept.at[:, k, pl.ds(OFF, T), :], local_sem.at[len(gets)]
            )
            copy.start()
            gets.append(copy)
    my_shift = (sh_ref[0, 0, 0], sh_ref[0, 0, 1])
    sub8 = lax.broadcasted_iota(jnp.int32, (8, 128), 0)
    shs[...] = jnp.where(sub8 == 0, my_shift[0], my_shift[1])

    for direction in DIRECTIONS:
        @pl.when(jnp.logical_not(present[direction]))
        def _():
            n = DIRECTIONS.index(direction)
            shr[n] = jnp.zeros((8, 128), jnp.int32)
            cr[n] = jnp.zeros((2, 8, 128), F32)
            kr[n] = jnp.zeros((16, 128), F32)
            if direction[0] == 0:
                er[0 if direction[1] > 0 else 1] = jnp.zeros((T // 2, 128), F32)
            if direction[1] == 0:
                base = OFF - 8 if direction[0] < 0 else OFF + T
                f1v[:, :, base:base + 8, :] = jnp.zeros((BANDS, 2, 8, 128), F32)

    sends = []

    def send(src, dst, direction):
        slot = len(sends)
        copy = pltpu.make_async_remote_copy(
            src_ref=src, dst_ref=dst, send_sem=send_sem.at[slot], recv_sem=recv_sem.at[slot],
            device_id=device(direction), device_id_type=pl.DeviceIdType.MESH,
        )
        sends.append((copy, direction))

    def start(copies):
        for direction in DIRECTIONS:
            @pl.when(present[direction])
            def _():
                for copy, way in copies:
                    if way == direction:
                        copy.start()

    def finish(copies):
        for direction in DIRECTIONS:
            ours = [copy for copy, way in copies if way == direction]
            if ours:
                @pl.when(present[direction])
                def _():
                    for copy in ours:
                        copy.wait_send()

                @pl.when(present[-direction[0], -direction[1]])
                def _():
                    for copy in ours:
                        copy.wait_recv()

    lane = lax.broadcasted_iota(jnp.int32, (8, 128), 1)
    place = lane % 16
    right_side = lane < 64
    tall = lax.broadcasted_iota(jnp.int32, (T // 2, 128), 1) < 64
    for copy in gets:
        copy.wait()

    def packing(i, carry):
        rows = aligned(OFF + 8 * i)
        acc = jnp.zeros((8, 128), F32)
        for b in range(BANDS):
            left2, right2, left1, right1 = s2[b, 0, rows, :], s2[b, 1, rows, :], f1v[b, 0, rows, :], f1v[b, 1, rows, :]
            left = jnp.where(place < 6, roll(left1, 16 * b, 1), roll(left2, 16 * b + 6, 1))
            right = jnp.where(place < 10, roll(right2, 16 * b + 74, 1), roll(right1, 16 * b + 78, 1))
            acc = jnp.where(lane // 16 == b, left, jnp.where(lane // 16 == b + 4, right, acc))
        pack[aligned(8 * i), :] = acc
        return carry

    lax.fori_loop(0, T // 8, packing, 0, unroll=32)
    upper, lower = pack[0:128, :], pack[128:256, :]
    es[0] = jnp.where(tall, upper, roll(lower, 64, 1))
    es[1] = jnp.where(tall, roll(upper, 64, 1), lower)

    pl.semaphore_wait(barrier, sum(here.astype(jnp.int32) for here in present.values()))

    for dr, dc in DIRECTIONS:
        seen = DIRECTIONS.index((-dr, -dc))
        if dr != 0 and dc != 0:
            send(pack.at[pl.ds(0 if dr < 0 else T - 16, 16), :], kr.at[seen], (dr, dc))
        elif dr == 0:
            side = 0 if dc < 0 else 1
            send(es.at[side], er.at[side], (dr, dc))
        else:
            from2, to2 = (OFF, OFF + T) if dr < 0 else (OFF + T - DEEP, OFF - DEEP)
            from1, to1 = (OFF, OFF + T) if dr < 0 else (OFF + T - THIN, OFF - THIN)
            both = pl.ds(0, 2)
            send(s2.at[:, both, pl.ds(from2, DEEP), :], s2.at[:, both, pl.ds(to2, DEEP), :], (dr, dc))
            send(f1v.at[:, both, pl.ds(from1, THIN), :], f1v.at[:, both, pl.ds(to1, THIN), :], (dr, dc))
        send(shs, shr.at[seen], (dr, dc))
    raw_sends = list(sends)
    start(raw_sends)

    col_id = lax.broadcasted_iota(jnp.int32, (128, 128), 0) // FACTOR
    lane_id = lax.broadcasted_iota(jnp.int32, (128, 128), 1)
    row_sum = (
        lax.broadcasted_iota(jnp.int32, (CT, T), 1) // FACTOR == lax.broadcasted_iota(jnp.int32, (CT, T), 0)
    ).astype(F32).astype(BF16)
    for frame in range(2):
        total = jnp.zeros((T, 128), F32)
        for b in range(BANDS):
            for k in range(2):
                block = (f1v if frame == 0 else s2)[b, k, OFF:OFF + T, :]
                weights = jnp.where(lane_id - CT * b - 16 * k == col_id, 1.0 / 64.0, 0.0).astype(BF16)
                total = total + dot_split(block, weights, 2)
        hi, mid, _ = split3(total)
        ce[frame, 8:8 + CT, :] = (
            jnp.dot(row_sum, hi, preferred_element_type=F32) + jnp.dot(row_sum, mid, preferred_element_type=F32)
        )
    group = (lax.broadcasted_iota(jnp.int32, (16, 128), 1) % CT) // 8
    edge_l = edge_r = jnp.zeros((16, 128), F32)
    for frame in range(2):
        for half in range(2):
            n = 2 * frame + half
            piece = ce[frame, 8 + 16 * half:24 + 16 * half, :]
            edge_l = jnp.where(group == n, roll(piece, 8 * n, 1), edge_l)
            edge_r = jnp.where(group == n, roll(piece, 8 * n - 24, 1), edge_r)
    for half in range(2):
        cs[0, half] = edge_l[8 * half:8 * half + 8]
        cs[1, half] = edge_r[8 * half:8 * half + 8]

    for dr, dc in DIRECTIONS:
        seen = DIRECTIONS.index((-dr, -dc))
        if dr == 0:
            send(cs.at[0 if dc < 0 else 1], cr.at[seen], (dr, dc))
        else:
            send(ce.at[:, pl.ds(8 if dr < 0 else CT, 8), :], cr.at[seen], (dr, dc))
    coarse_sends = sends[len(raw_sends):]
    start(coarse_sends)

    def own_edge(start):
        acc = jnp.zeros((8, 128), F32)
        for b in range(BANDS):
            left, right = s2[b, 0, aligned(start), :], s2[b, 1, aligned(start), :]
            acc = jnp.where(lane // 16 == b, roll(right, 16 * b + 6, 1), acc)
            acc = jnp.where(lane // 16 == b + 4, roll(left, 16 * b + 74, 1), acc)
        return acc

    def owning(i, carry):
        own[aligned(OFF + 8 * i), :] = own_edge(OFF + 8 * i)
        return carry

    lax.fori_loop(0, T // 8, owning, 0, unroll=8)

    finish([(copy, way) for copy, way in raw_sends if 0 in way])

    def at(direction):
        return DIRECTIONS.index(direction)

    def shift_at(d):
        return shr[at(d), 0, 0], shr[at(d), 1, 0]

    keep_lane = jnp.where(
        lane[0:1] < 64, jnp.where(me_c == n_c - 1, 0.0, 1.0), jnp.where(me_c == 0, 0.0, 1.0)
    )
    eq[OFF:OFF + 128, :] = jnp.where(tall, er[0], roll(er[1], 64, 1)) * keep_lane
    eq[OFF + 128:OFF + 256, :] = jnp.where(tall, roll(er[0], 64, 1), er[1]) * keep_lane

    @pl.when(me_r == 0)
    def _():
        s2[:, 0:2, OFF - 16:OFF, :] = jnp.zeros((BANDS, 2, 16, 128), F32)

    @pl.when(me_r == n_r - 1)
    def _():
        s2[:, 0:2, OFF + T:OFF + T + 16, :] = jnp.zeros((BANDS, 2, 16, 128), F32)

    for start in (OFF - 16, OFF - 8, OFF + T, OFF + T + 8):
        own[start:start + 8, :] = own_edge(start)

    theirs = (right_side & (place >= 6)) | ((lane >= 64) & (place < 10))

    def third(i, carry):
        rows = aligned(OFF - 16 + 8 * i)
        x = eq[rows, :]
        mix = jnp.where((place >= 6) & (place < 13), x, roll(x, 60, 1))
        for b in range(BANDS):
            s2[b, 2, rows, :] = roll(mix, -(16 * b + 6), 1)
        own[rows, :] = jnp.where(theirs, x, own[rows, :])
        return carry

    lax.fori_loop(2, STRIPS, third, 0, unroll=16)

    panel_lane = lax.broadcasted_iota(jnp.int32, (PANELS, 8, 128), 2)

    def back(shift):
        return jnp.where(shift > 0, 128 - shift, -shift)

    def store_data(fields, b, panels, rows, pull):
        dr, dc, wf = fields
        first = jnp.clip(wf, -LAM, LAM)
        g[b, panels, rows, :] = dr
        g[BANDS + b, panels, rows, :] = dc
        g[2 * BANDS + b, panels, rows, :] = wf
        a[b, panels, rows, :] = first + wf
        return [pull[0] + first * dr, pull[1] + first * dc]

    def window(base, shift):
        rows = aligned(base)
        start = base + shift[0]
        amount = back(shift[1])
        over = panel_lane + shift[1] >= 128
        under = panel_lane + shift[1] < 0

        def shifted(x):
            turned = pltpu.roll(x, amount, 2)
            return jnp.where(over, following(turned), jnp.where(under, preceding(turned), turned))

        pull = [0.0, 0.0]
        for b in range(BANDS):
            here = shifted(s2[b, :, pl.ds(start, 8), :])
            down = shifted(s2[b, :, pl.ds(start + 1, 8), :] - s2[b, :, pl.ds(start - 1, 8), :])
            fields = (down[:2], across(here)[:2], SIGMA * (here[:2] - f1v[b, :, rows, :]))
            pull = store_data(fields, b, slice(0, 2), rows, pull)
        for c in range(2):
            p1[c, 0:2, rows, :] = pull[c]

    amount = back(my_shift[1])
    over = panel_lane + my_shift[1] >= 128
    under = panel_lane + my_shift[1] < 0

    def moving(s, carry):
        base = FIRST + 8 * s
        for b in range(BANDS):
            turned = pltpu.roll(s2[b, :, pl.ds(base + my_shift[0], 8), :], amount, 2)
            wv[b, :, aligned(base), :] = jnp.where(
                over, following(turned), jnp.where(under, preceding(turned), turned)
            )
        return carry

    lax.fori_loop(1, STRIPS - 1, moving, 0, unroll=MOVE)

    def window_loop(i, carry):
        base = OFF + 8 * i
        rows = aligned(base)
        pull = [0.0, 0.0]
        for b in range(BANDS):
            here = wv[b, :, rows, :]
            fields = (
                wv[b, 0:2, pl.ds(base + 1, 8), :] - wv[b, 0:2, pl.ds(base - 1, 8), :],
                across(here)[:2],
                SIGMA * (here[:2] - f1v[b, :, rows, :]),
            )
            pull = store_data(fields, b, slice(0, 2), rows, pull)
        for c in range(2):
            p1[c, 0:2, rows, :] = pull[c]
        return carry

    lax.fori_loop(1, T // 8 - 1, window_loop, 0, unroll=10)

    def edge(base, right, left):
        rows = aligned(base)

        def pick(x, y):
            return jnp.where(right_side, pltpu.roll(x, back(right[1]), 1), pltpu.roll(y, back(left[1]), 1))

        def near(shift, step):
            return own[pl.ds(base + shift[0] + step, 8), :]

        here = pick(near(right, 0), near(left, 0))
        down = pick(near(right, 1) - near(right, -1), near(left, 1) - near(left, -1))
        x = eq[rows, :]
        first = jnp.where(right_side, roll(x, 6, 1), roll(x, -4, 1))
        kinds = []
        for field in (down, next_minus_prev(here, 1), SIGMA * (here - first)):
            kinds.append(jnp.where((place >= 6) & (place < 10), field, roll(field, 60, 1)))
        pull = [0.0, 0.0]
        for b in range(BANDS):
            fields = [roll(kind, -(16 * b + 6), 1) for kind in kinds]
            pull = store_data(fields, b, 2, rows, pull)
        for c in range(2):
            p1[c, 2, rows, :] = pull[c]

    side_shifts = shift_at((0, 1)), shift_at((0, -1))

    def edge_loop(i, carry):
        edge(OFF + 8 * i, *side_shifts)
        return carry

    lax.fori_loop(1, T // 8 - 1, edge_loop, 0, unroll=EDGE)

    finish([(copy, way) for copy, way in raw_sends if 0 not in way])
    keep_above = jnp.where(me_r == 0, 0.0, 1.0) * keep_lane
    keep_below = jnp.where(me_r == n_r - 1, 0.0, 1.0) * keep_lane
    side16 = lax.broadcasted_iota(jnp.int32, (16, 128), 1) < 64
    eq[OFF - 16:OFF, :] = jnp.where(side16, kr[at((-1, 1))], kr[at((-1, -1))]) * keep_above
    eq[OFF + T:OFF + T + 16, :] = jnp.where(side16, kr[at((1, 1))], kr[at((1, -1))]) * keep_below
    for i in (0, 1, STRIPS, STRIPS + 1):
        third(i, 0)

    def outermost(j, carry):
        moving(j * (STRIPS - 1), 0)
        moving(j * (STRIPS - 3) + 1, 0)
        return carry

    lax.fori_loop(0, 2, outermost, 0, unroll=2)
    lax.fori_loop(0, 2, lambda j, carry: window_loop(j * (T // 8 - 1), carry), 0, unroll=2)
    window(OFF - 8, shift_at((-1, 0)))
    window(OFF + T, shift_at((1, 0)))
    lax.fori_loop(0, 2, lambda j, carry: edge_loop(j * (T // 8 - 1), carry), 0, unroll=2)
    edge(OFF - 8, shift_at((-1, 1)), shift_at((-1, -1)))
    edge(OFF + T, shift_at((1, 1)), shift_at((1, -1)))

    crow = lax.broadcasted_iota(jnp.int32, (CROWS, 128), 0) - 8 + me_r * CT
    clane = lax.broadcasted_iota(jnp.int32, (CROWS, 128), 1)
    ccol = jnp.where(clane < 64, clane, clane - 128) + me_c * CT
    mask = jnp.where((crow >= 0) & (crow < n_r * CT) & (ccol >= 0) & (ccol < n_c * CT), 1.0, 0.0)
    finish(coarse_sends)
    means = []
    for frame in range(2):
        def column(dc):
            parts = [cr[at((-1, dc)), frame]]
            turn = CT * dc
            if dc == 0:
                parts.append(ce[frame, 8:8 + CT, :])
            else:
                for half in range(2):
                    n = 2 * frame + half
                    side = cr[at((0, dc))]
                    side = jnp.concatenate([side[0], side[1]], axis=0)
                    parts.append(roll(side, (0 if dc > 0 else 24) - 8 * n, 1))
            parts.append(cr[at((1, dc)), frame])
            return roll(jnp.concatenate(parts, axis=0), turn, 1)

        mine, right, left = column(0), column(1), column(-1)
        bands = []
        for b in range(BANDS):
            mix = jnp.where(clane // CT == (b + 1) % 4, right, jnp.where(clane // CT == (b + 3) % 4, left, mine))
            bands.append(roll(mix, -CT * b, 1) * mask)
        means.append(bands)
    grad_r = [0.5 * next_minus_prev(x, 0) for x in means[1]]
    grad_c = [0.5 * next_minus_prev(x, 1) for x in means[1]]
    off = [means[1][b] - means[0][b] for b in range(BANDS)]
    now = [jnp.zeros((CROWS, 128), F32)] * 2
    bar = now
    dual_r, dual_c = list(now), list(now)
    data = [jnp.zeros((CROWS, 128), F32)] * BANDS
    for it in range(3):
        div = [0.0, 0.0]
        if it > 0:
            for c in range(2):
                pr = dual_r[c] + (0.5 * SIGMA) * next_minus_prev(bar[c], 0)
                pc = dual_c[c] + (0.5 * SIGMA) * next_minus_prev(bar[c], 1)
                k = shrink(pr * pr + pc * pc) * mask
                dual_r[c], dual_c[c] = pr * k, pc * k
                div[c] = 0.5 * (next_minus_prev(dual_r[c], 0) + next_minus_prev(dual_c[c], 1))
        pull = [0.0, 0.0]
        for b in range(BANDS):
            rho = off[b]
            if it > 0:
                rho = rho + grad_r[b] * bar[0] + grad_c[b] * bar[1]
            data[b] = jnp.clip(data[b] + SIGMA * rho, -LAM, LAM)
            pull = [pull[0] + data[b] * grad_r[b], pull[1] + data[b] * grad_c[b]]
        later = [(now[c] + TAU * (div[c] - pull[c])) * mask for c in range(2)]
        bar = [2.0 * later[c] - now[c] for c in range(2)]
        now = later
    for c in range(2):
        coarse_ref[c] = now[c][8:8 + CT, 0:CT]

    wide_shape = (128, 128 * PANELS)
    wide = lax.broadcasted_iota(jnp.int32, wide_shape, 1)
    source = jnp.where(wide < T + 64, wide // FACTOR, 128 - (128 * PANELS - wide + FACTOR - 1) // FACTOR)
    spread = jnp.where(lax.broadcasted_iota(jnp.int32, wide_shape, 0) == source, 1.0, 0.0).astype(BF16)
    block_lane = lax.broadcasted_iota(jnp.int32, (PANELS, CROWS, 128), 2)
    block_lane = block_lane + 128 * lax.broadcasted_iota(jnp.int32, (PANELS, CROWS, 128), 0)
    block_row = lax.broadcasted_iota(jnp.int32, (PANELS, CROWS, 128), 1) - 8 + me_r * CT
    block_col = jnp.where(block_lane < T + 64, block_lane, block_lane - 128 * PANELS) + me_c * T
    block_mask = jnp.where(
        (block_row >= 0) & (block_row < n_r * CT) & (block_col >= 0) & (block_col < n_c * T), 1.0, 0.0
    )
    for c in range(2):
        repeated = dot_split(now[c], spread, 3)
        t = jnp.stack([repeated[:, 128 * k:128 * k + 128] for k in range(PANELS)])
        first_r = t - roll(t, 1, 1)
        last_r = roll(t, -1, 1) - t
        step_c = across(t)
        square = step_c * step_c
        k_first = shrink(first_r * first_r + square) * block_mask
        k_inner = shrink(square) * block_mask
        k_last = shrink(last_r * last_r + square) * block_mask
        pr_first, pr_last = first_r * k_first, last_r * k_last
        pc_first, pc_inner, pc_last = step_c * k_first, step_c * k_inner, step_c * k_last
        inner = across(pc_inner)
        for n, value in enumerate((
            t, pr_first, pr_last, pc_first, pc_inner, pc_last,
            across(pc_first) - roll(pr_last, 1, 1), inner - pr_first, inner, inner + pr_last,
            across(pc_last) + roll(pr_first, -1, 1),
        )):
            tc[n, c] = value

    def block_row_of(n, c, s):
        return jnp.broadcast_to(tc[n, c, :, pl.ds(s + 7, 1), :], (PANELS, 8, 128))

    panel_sub = lax.broadcasted_iota(jnp.int32, (PANELS, 8, 128), 1)
    right_in = jnp.where(me_c == n_c - 1, 0.0, 1.0)
    left_in = jnp.where(me_c == 0, 0.0, 1.0)
    col_mask = jnp.where(panel_lane[:1] < 64, right_in, left_in)

    def inside_cols(x):
        return jnp.concatenate([x[:2], x[2:] * col_mask], axis=0)

    def clear_rows(ref):
        @pl.when(me_r == 0)
        def _():
            ref[:, :, FIRST:FIRST + 8, :] = jnp.zeros((2, PANELS, 8, 128), F32)

        @pl.when(me_r == n_r - 1)
        def _():
            ref[:, :, OFF + T:OFF + T + 8, :] = jnp.zeros((2, PANELS, 8, 128), F32)

    def opening(s, carry):
        rows = aligned(FIRST + 8 * s)
        for c in range(2):
            t, pr_first, pr_last, pc_first, pc_inner, pc_last, d0, d1, dm, d6, d7 = [
                block_row_of(n, c, s) for n in range(11)
            ]
            at0, at7 = panel_sub == 0, panel_sub == 7
            div = jnp.where(at0, d0, jnp.where(at7, d7, jnp.where(panel_sub == 1, d1, jnp.where(panel_sub == 6, d6, dm))))
            prv[c, :, rows, :] = jnp.where(at0, pr_first, jnp.where(at7, pr_last, 0.0))
            pcv[c, :, rows, :] = jnp.where(at0, pc_first, jnp.where(at7, pc_last, pc_inner))
            later = t + (1.0 / 64.0) * (div - p1[c, :, rows, :])
            u[c, :, rows, :] = later
            ub[c, :, rows, :] = inside_cols(2.0 * later - t)
        return carry

    lax.fori_loop(0, STRIPS, opening, 0, unroll=UNROLL)
    clear_rows(ub)

    for it in (1, 2):
        def dual(s, carry):
            base = FIRST + 8 * s
            rows = aligned(base)
            for c in range(2):
                pr = prv[c, :, rows, :] + (ub[c, :, pl.ds(base + 1, 8), :] - ub[c, :, pl.ds(base - 1, 8), :])
                pc = pcv[c, :, rows, :] + across(ub[c, :, rows, :])
                k = inside_cols(shrink(pr * pr + pc * pc))
                prv[c, :, rows, :] = pr * k
                pcv[c, :, rows, :] = pc * k
            return carry

        lax.fori_loop(0, STRIPS, dual, 0, unroll=UNROLL)
        clear_rows(prv)

        def primal(s, carry):
            base = FIRST + 8 * s
            rows = aligned(base)
            n = PANELS if it < 2 else 2
            step = [(ub[c, :, rows, :] - block_row_of(0, c, s))[:n] for c in range(2)]
            pull = [0.0, 0.0]
            for b in range(BANDS):
                gr, gc = g[b, 0:n, rows, :], g[BANDS + b, 0:n, rows, :]
                value = a[b, 0:n, rows, :] + gr * step[0] + gc * step[1]
                if it == 2:
                    value = value + g[2 * BANDS + b, 0:n, rows, :]
                value = jnp.clip(value, -LAM, LAM)
                if it < 2:
                    a[b, :, rows, :] = value
                pull = [pull[0] + value * gr, pull[1] + value * gc]
            for c in range(2):
                div = (
                    prv[c, 0:n, pl.ds(base + 1, 8), :] - prv[c, 0:n, pl.ds(base - 1, 8), :]
                    + across(pcv[c, :, rows, :])[:n]
                )
                was = u[c, 0:n, rows, :]
                later = was + (1.0 / 64.0) * (div - pull[c])
                if it < 2:
                    u[c, :, rows, :] = later
                    ub[c, :, rows, :] = inside_cols(2.0 * later - was)
                else:
                    for k in range(2):
                        flow_ref[c, aligned(base - OFF), 128 * k:128 * k + 128] = 8.0 * later[k]
            return carry

        if it < 2:
            lax.fori_loop(0, STRIPS, primal, 0, unroll=UNROLL)
            clear_rows(ub)
        else:
            lax.fori_loop(1, STRIPS - 1, primal, 0, unroll=16)


def local(frame_first, frame_second, shifts):
    vmem = pltpu.VMEM
    field = vmem((2, PANELS, ROWS, 128), F32)
    return pl.pallas_call(
        kernel,
        out_shape=(
            vmem((2, T, T), F32),
            vmem((2, CT, CT), F32),
        ),
        in_specs=[
            pl.BlockSpec(memory_space=pl.ANY),
            pl.BlockSpec(memory_space=pl.ANY),
            pl.BlockSpec(memory_space=pltpu.SMEM),
        ],
        out_specs=(pl.BlockSpec(memory_space=vmem), pl.BlockSpec(memory_space=vmem)),
        scratch_shapes=[
            vmem((BANDS, PANELS, ROWS, 128), F32),
            vmem((BANDS, PANELS, ROWS, 128), F32),
            vmem((BANDS, 2, ROWS, 128), F32),
            vmem((3 * BANDS, PANELS, ROWS, 128), F32),
            vmem((BANDS, PANELS, ROWS, 128), F32),
            field, field, field, field, field,
            vmem((11, 2, PANELS, CROWS, 128), F32),
            vmem((2, CROWS, 128), F32),
            vmem((2, 2, 8, 128), F32),
            vmem((8, 2, 8, 128), F32),
            vmem((T, 128), F32),
            vmem((2, T // 2, 128), F32),
            vmem((2, T // 2, 128), F32),
            vmem((8, 16, 128), F32),
            vmem((ROWS, 128), F32),
            vmem((ROWS, 128), F32),
            vmem((8, 128), jnp.int32),
            vmem((8, 8, 128), jnp.int32),
            pltpu.SemaphoreType.DMA((4,)),
            pltpu.SemaphoreType.DMA((32,)),
            pltpu.SemaphoreType.DMA((32,)),
        ],
        compiler_params=pltpu.CompilerParams(
            collective_id=0, has_side_effects=True, vmem_limit_bytes=60 * 1024 * 1024
        ),
    )(frame_first, frame_second, shifts)


def solution(mesh):
    return jax.shard_map(
        local,
        mesh=mesh,
        in_specs=(P(None, "row", "col"), P(None, "row", "col"), P("row", "col", None)),
        out_specs=(P(None, "row", "col"), P(None, "row", "col")),
        check_vma=False,
    )
```

```python
import jax
import jax.numpy as jnp
from jax import lax
from jax.experimental import pallas as pl
from jax.experimental.pallas import tpu as pltpu
from jax.sharding import PartitionSpec as P

FACTOR = 8
TAU = 0.25
SIGMA = 0.25
LAM = 0.3
ALPHA = 0.3
BANDS = 4
T = 256
CT = T // FACTOR
OFF = 24
ROWS = T + 2 * OFF
FIRST = OFF - 8
STRIPS = T // 8 + 2
UNROLL = STRIPS
MOVE = 16
EDGE = 10
PANELS = 3
DEEP = 9
THIN = 4
CROWS = CT + 16
F32 = jnp.float32
BF16 = jnp.bfloat16
DIRECTIONS = [(0, -1), (0, 1), (-1, -1), (-1, 1), (1, -1), (1, 1), (-1, 0), (1, 0)]


def split3(x):
    hi = x.astype(BF16)
    rest = x - hi.astype(F32)
    mid = rest.astype(BF16)
    low = (rest - mid.astype(F32)).astype(BF16)
    return hi, mid, low


def dot_split(x, w, parts):
    total = None
    for piece in split3(x)[:parts]:
        term = jnp.dot(piece, w, preferred_element_type=F32)
        total = term if total is None else total + term
    return total


def roll(x, amount, axis):
    amount = amount % x.shape[axis]
    return x if amount == 0 else pltpu.roll(x, amount, axis)


def next_minus_prev(x, axis):
    return roll(x, -1, axis) - roll(x, 1, axis)


def following(x):
    return jnp.concatenate([x[1:], x[:1]], axis=0)


def preceding(x):
    return jnp.concatenate([x[-1:], x[:-1]], axis=0)


def across(x):
    lane = lax.broadcasted_iota(jnp.int32, x.shape, 2)
    ahead, behind = roll(x, -1, 2), roll(x, 1, 2)
    return jnp.where(lane == 127, following(ahead), ahead) - jnp.where(lane == 0, preceding(behind), behind)


def shrink(square):
    return jnp.minimum(1.0, ALPHA * lax.rsqrt(square))


def aligned(start, size=8):
    return pl.ds(pl.multiple_of(start, 8), size)


def kernel(
    f1_ref, f2_ref, sh_ref, flow_ref, coarse_ref,
    s2, wv, f1v, g, a, p1, u, ub, prv, pcv, tc, ce, cs, cr,
    pack, es, er, kr, eq, own, shs, shr,
    local_sem, send_sem, recv_sem,
):
    me_r, me_c = lax.axis_index("row"), lax.axis_index("col")
    n_r, n_c = lax.axis_size("row"), lax.axis_size("col")

    def device(direction):
        dr, dc = direction
        return (lax.rem(me_r + dr + n_r, n_r), lax.rem(me_c + dc + n_c, n_c))

    def exists(direction):
        row, col = me_r + direction[0], me_c + direction[1]
        return (row >= 0) & (row < n_r) & (col >= 0) & (col < n_c)

    present = {d: exists(d) for d in DIRECTIONS}
    barrier = pltpu.get_barrier_semaphore()
    for direction in DIRECTIONS:
        @pl.when(present[direction])
        def _():
            pl.semaphore_signal(barrier, inc=1, device_id=device(direction), device_id_type=pl.DeviceIdType.MESH)
    gets = []
    for ref, kept in ((f2_ref, s2), (f1_ref, f1v)):
        for k in range(2):
            copy = pltpu.make_async_copy(
                ref.at[:, :, pl.ds(128 * k, 128)], kept.at[:, k, pl.ds(OFF, T), :], local_sem.at[len(gets)]
            )
            copy.start()
            gets.append(copy)
    my_shift = (sh_ref[0, 0, 0], sh_ref[0, 0, 1])
    sub8 = lax.broadcasted_iota(jnp.int32, (8, 128), 0)
    shs[...] = jnp.where(sub8 == 0, my_shift[0], my_shift[1])

    for direction in DIRECTIONS:
        @pl.when(jnp.logical_not(present[direction]))
        def _():
            n = DIRECTIONS.index(direction)
            shr[n] = jnp.zeros((8, 128), jnp.int32)
            cr[n] = jnp.zeros((2, 8, 128), F32)
            kr[n] = jnp.zeros((16, 128), F32)
            if direction[0] == 0:
                er[0 if direction[1] > 0 else 1] = jnp.zeros((T // 2, 128), F32)
            if direction[1] == 0:
                base = OFF - 8 if direction[0] < 0 else OFF + T
                f1v[:, :, base:base + 8, :] = jnp.zeros((BANDS, 2, 8, 128), F32)

    sends = []

    def send(src, dst, direction):
        slot = len(sends)
        copy = pltpu.make_async_remote_copy(
            src_ref=src, dst_ref=dst, send_sem=send_sem.at[slot], recv_sem=recv_sem.at[slot],
            device_id=device(direction), device_id_type=pl.DeviceIdType.MESH,
        )
        sends.append((copy, direction))

    def start(copies):
        for direction in DIRECTIONS:
            @pl.when(present[direction])
            def _():
                for copy, way in copies:
                    if way == direction:
                        copy.start()

    def finish(copies):
        for direction in DIRECTIONS:
            ours = [copy for copy, way in copies if way == direction]
            if ours:
                @pl.when(present[direction])
                def _():
                    for copy in ours:
                        copy.wait_send()

                @pl.when(present[-direction[0], -direction[1]])
                def _():
                    for copy in ours:
                        copy.wait_recv()

    lane = lax.broadcasted_iota(jnp.int32, (8, 128), 1)
    place = lane % 16
    right_side = lane < 64
    tall = lax.broadcasted_iota(jnp.int32, (T // 2, 128), 1) < 64
    for copy in gets:
        copy.wait()

    def packing(i, carry):
        rows = aligned(OFF + 8 * i)
        acc = jnp.zeros((8, 128), F32)
        for b in range(BANDS):
            left2, right2, left1, right1 = s2[b, 0, rows, :], s2[b, 1, rows, :], f1v[b, 0, rows, :], f1v[b, 1, rows, :]
            left = jnp.where(place < 6, roll(left1, 16 * b, 1), roll(left2, 16 * b + 6, 1))
            right = jnp.where(place < 10, roll(right2, 16 * b + 74, 1), roll(right1, 16 * b + 78, 1))
            acc = jnp.where(lane // 16 == b, left, jnp.where(lane // 16 == b + 4, right, acc))
        pack[aligned(8 * i), :] = acc
        return carry

    lax.fori_loop(0, T // 8, packing, 0, unroll=32)
    upper, lower = pack[0:128, :], pack[128:256, :]
    es[0] = jnp.where(tall, upper, roll(lower, 64, 1))
    es[1] = jnp.where(tall, roll(upper, 64, 1), lower)

    pl.semaphore_wait(barrier, sum(here.astype(jnp.int32) for here in present.values()))

    for dr, dc in DIRECTIONS:
        seen = DIRECTIONS.index((-dr, -dc))
        if dr != 0 and dc != 0:
            send(pack.at[pl.ds(0 if dr < 0 else T - 16, 16), :], kr.at[seen], (dr, dc))
        elif dr == 0:
            side = 0 if dc < 0 else 1
            send(es.at[side], er.at[side], (dr, dc))
        else:
            from2, to2 = (OFF, OFF + T) if dr < 0 else (OFF + T - DEEP, OFF - DEEP)
            from1, to1 = (OFF, OFF + T) if dr < 0 else (OFF + T - THIN, OFF - THIN)
            both = pl.ds(0, 2)
            send(s2.at[:, both, pl.ds(from2, DEEP), :], s2.at[:, both, pl.ds(to2, DEEP), :], (dr, dc))
            send(f1v.at[:, both, pl.ds(from1, THIN), :], f1v.at[:, both, pl.ds(to1, THIN), :], (dr, dc))
        send(shs, shr.at[seen], (dr, dc))
    raw_sends = list(sends)
    start(raw_sends)

    col_id = lax.broadcasted_iota(jnp.int32, (128, 128), 0) // FACTOR
    lane_id = lax.broadcasted_iota(jnp.int32, (128, 128), 1)
    row_sum = (
        lax.broadcasted_iota(jnp.int32, (CT, T), 1) // FACTOR == lax.broadcasted_iota(jnp.int32, (CT, T), 0)
    ).astype(F32).astype(BF16)
    for frame in range(2):
        total = jnp.zeros((T, 128), F32)
        for b in range(BANDS):
            for k in range(2):
                block = (f1v if frame == 0 else s2)[b, k, OFF:OFF + T, :]
                weights = jnp.where(lane_id - CT * b - 16 * k == col_id, 1.0 / 64.0, 0.0).astype(BF16)
                total = total + dot_split(block, weights, 2)
        hi, mid, _ = split3(total)
        ce[frame, 8:8 + CT, :] = (
            jnp.dot(row_sum, hi, preferred_element_type=F32) + jnp.dot(row_sum, mid, preferred_element_type=F32)
        )
    group = (lax.broadcasted_iota(jnp.int32, (16, 128), 1) % CT) // 8
    edge_l = edge_r = jnp.zeros((16, 128), F32)
    for frame in range(2):
        for half in range(2):
            n = 2 * frame + half
            piece = ce[frame, 8 + 16 * half:24 + 16 * half, :]
            edge_l = jnp.where(group == n, roll(piece, 8 * n, 1), edge_l)
            edge_r = jnp.where(group == n, roll(piece, 8 * n - 24, 1), edge_r)
    for half in range(2):
        cs[0, half] = edge_l[8 * half:8 * half + 8]
        cs[1, half] = edge_r[8 * half:8 * half + 8]

    for dr, dc in DIRECTIONS:
        seen = DIRECTIONS.index((-dr, -dc))
        if dr == 0:
            send(cs.at[0 if dc < 0 else 1], cr.at[seen], (dr, dc))
        else:
            send(ce.at[:, pl.ds(8 if dr < 0 else CT, 8), :], cr.at[seen], (dr, dc))
    coarse_sends = sends[len(raw_sends):]
    start(coarse_sends)

    def own_edge(start):
        acc = jnp.zeros((8, 128), F32)
        for b in range(BANDS):
            left, right = s2[b, 0, aligned(start), :], s2[b, 1, aligned(start), :]
            acc = jnp.where(lane // 16 == b, roll(right, 16 * b + 6, 1), acc)
            acc = jnp.where(lane // 16 == b + 4, roll(left, 16 * b + 74, 1), acc)
        return acc

    def owning(i, carry):
        own[aligned(OFF + 8 * i), :] = own_edge(OFF + 8 * i)
        return carry

    lax.fori_loop(0, T // 8, owning, 0, unroll=8)

    finish([(copy, way) for copy, way in raw_sends if 0 in way])

    def at(direction):
        return DIRECTIONS.index(direction)

    def shift_at(d):
        return shr[at(d), 0, 0], shr[at(d), 1, 0]

    keep_lane = jnp.where(
        lane[0:1] < 64, jnp.where(me_c == n_c - 1, 0.0, 1.0), jnp.where(me_c == 0, 0.0, 1.0)
    )
    eq[OFF:OFF + 128, :] = jnp.where(tall, er[0], roll(er[1], 64, 1)) * keep_lane
    eq[OFF + 128:OFF + 256, :] = jnp.where(tall, roll(er[0], 64, 1), er[1]) * keep_lane

    @pl.when(me_r == 0)
    def _():
        s2[:, 0:2, OFF - 16:OFF, :] = jnp.zeros((BANDS, 2, 16, 128), F32)

    @pl.when(me_r == n_r - 1)
    def _():
        s2[:, 0:2, OFF + T:OFF + T + 16, :] = jnp.zeros((BANDS, 2, 16, 128), F32)

    for start in (OFF - 16, OFF - 8, OFF + T, OFF + T + 8):
        own[start:start + 8, :] = own_edge(start)

    theirs = (right_side & (place >= 6)) | ((lane >= 64) & (place < 10))

    def third(i, carry):
        rows = aligned(OFF - 16 + 8 * i)
        x = eq[rows, :]
        mix = jnp.where((place >= 6) & (place < 13), x, roll(x, 60, 1))
        for b in range(BANDS):
            s2[b, 2, rows, :] = roll(mix, -(16 * b + 6), 1)
        own[rows, :] = jnp.where(theirs, x, own[rows, :])
        return carry

    lax.fori_loop(2, STRIPS, third, 0, unroll=16)

    panel_lane = lax.broadcasted_iota(jnp.int32, (PANELS, 8, 128), 2)

    def back(shift):
        return jnp.where(shift > 0, 128 - shift, -shift)

    def store_data(fields, b, panels, rows, pull):
        dr, dc, wf = fields
        first = jnp.clip(wf, -LAM, LAM)
        g[b, panels, rows, :] = dr
        g[BANDS + b, panels, rows, :] = dc
        g[2 * BANDS + b, panels, rows, :] = wf
        a[b, panels, rows, :] = first + wf
        return [pull[0] + first * dr, pull[1] + first * dc]

    def window(base, shift):
        rows = aligned(base)
        start = base + shift[0]
        amount = back(shift[1])
        over = panel_lane + shift[1] >= 128
        under = panel_lane + shift[1] < 0

        def shifted(x):
            turned = pltpu.roll(x, amount, 2)
            return jnp.where(over, following(turned), jnp.where(under, preceding(turned), turned))

        pull = [0.0, 0.0]
        for b in range(BANDS):
            here = shifted(s2[b, :, pl.ds(start, 8), :])
            down = shifted(s2[b, :, pl.ds(start + 1, 8), :] - s2[b, :, pl.ds(start - 1, 8), :])
            fields = (down[:2], across(here)[:2], SIGMA * (here[:2] - f1v[b, :, rows, :]))
            pull = store_data(fields, b, slice(0, 2), rows, pull)
        for c in range(2):
            p1[c, 0:2, rows, :] = pull[c]

    amount = back(my_shift[1])
    over = panel_lane + my_shift[1] >= 128
    under = panel_lane + my_shift[1] < 0

    def moving(s, carry):
        base = FIRST + 8 * s
        for b in range(BANDS):
            turned = pltpu.roll(s2[b, :, pl.ds(base + my_shift[0], 8), :], amount, 2)
            wv[b, :, aligned(base), :] = jnp.where(
                over, following(turned), jnp.where(under, preceding(turned), turned)
            )
        return carry

    lax.fori_loop(1, STRIPS - 1, moving, 0, unroll=MOVE)

    def window_loop(i, carry):
        base = OFF + 8 * i
        rows = aligned(base)
        pull = [0.0, 0.0]
        for b in range(BANDS):
            here = wv[b, :, rows, :]
            fields = (
                wv[b, 0:2, pl.ds(base + 1, 8), :] - wv[b, 0:2, pl.ds(base - 1, 8), :],
                across(here)[:2],
                SIGMA * (here[:2] - f1v[b, :, rows, :]),
            )
            pull = store_data(fields, b, slice(0, 2), rows, pull)
        for c in range(2):
            p1[c, 0:2, rows, :] = pull[c]
        return carry

    lax.fori_loop(1, T // 8 - 1, window_loop, 0, unroll=15)

    def edge(base, right, left):
        rows = aligned(base)

        def pick(x, y):
            return jnp.where(right_side, pltpu.roll(x, back(right[1]), 1), pltpu.roll(y, back(left[1]), 1))

        def near(shift, step):
            return own[pl.ds(base + shift[0] + step, 8), :]

        here = pick(near(right, 0), near(left, 0))
        down = pick(near(right, 1) - near(right, -1), near(left, 1) - near(left, -1))
        x = eq[rows, :]
        first = jnp.where(right_side, roll(x, 6, 1), roll(x, -4, 1))
        kinds = []
        for field in (down, next_minus_prev(here, 1), SIGMA * (here - first)):
            kinds.append(jnp.where((place >= 6) & (place < 10), field, roll(field, 60, 1)))
        pull = [0.0, 0.0]
        for b in range(BANDS):
            fields = [roll(kind, -(16 * b + 6), 1) for kind in kinds]
            pull = store_data(fields, b, 2, rows, pull)
        for c in range(2):
            p1[c, 2, rows, :] = pull[c]

    side_shifts = shift_at((0, 1)), shift_at((0, -1))

    def edge_loop(i, carry):
        edge(OFF + 8 * i, *side_shifts)
        return carry

    lax.fori_loop(1, T // 8 - 1, edge_loop, 0, unroll=EDGE)

    finish([(copy, way) for copy, way in raw_sends if 0 not in way])
    keep_above = jnp.where(me_r == 0, 0.0, 1.0) * keep_lane
    keep_below = jnp.where(me_r == n_r - 1, 0.0, 1.0) * keep_lane
    side16 = lax.broadcasted_iota(jnp.int32, (16, 128), 1) < 64
    eq[OFF - 16:OFF, :] = jnp.where(side16, kr[at((-1, 1))], kr[at((-1, -1))]) * keep_above
    eq[OFF + T:OFF + T + 16, :] = jnp.where(side16, kr[at((1, 1))], kr[at((1, -1))]) * keep_below
    for i in (0, 1, STRIPS, STRIPS + 1):
        third(i, 0)

    def outermost(j, carry):
        moving(j * (STRIPS - 1), 0)
        moving(j * (STRIPS - 3) + 1, 0)
        return carry

    lax.fori_loop(0, 2, outermost, 0, unroll=2)
    lax.fori_loop(0, 2, lambda j, carry: window_loop(j * (T // 8 - 1), carry), 0, unroll=2)
    window(OFF - 8, shift_at((-1, 0)))
    window(OFF + T, shift_at((1, 0)))
    lax.fori_loop(0, 2, lambda j, carry: edge_loop(j * (T // 8 - 1), carry), 0, unroll=2)
    edge(OFF - 8, shift_at((-1, 1)), shift_at((-1, -1)))
    edge(OFF + T, shift_at((1, 1)), shift_at((1, -1)))

    crow = lax.broadcasted_iota(jnp.int32, (CROWS, 128), 0) - 8 + me_r * CT
    clane = lax.broadcasted_iota(jnp.int32, (CROWS, 128), 1)
    ccol = jnp.where(clane < 64, clane, clane - 128) + me_c * CT
    mask = jnp.where((crow >= 0) & (crow < n_r * CT) & (ccol >= 0) & (ccol < n_c * CT), 1.0, 0.0)
    finish(coarse_sends)
    means = []
    for frame in range(2):
        def column(dc):
            parts = [cr[at((-1, dc)), frame]]
            turn = CT * dc
            if dc == 0:
                parts.append(ce[frame, 8:8 + CT, :])
            else:
                for half in range(2):
                    n = 2 * frame + half
                    side = cr[at((0, dc))]
                    side = jnp.concatenate([side[0], side[1]], axis=0)
                    parts.append(roll(side, (0 if dc > 0 else 24) - 8 * n, 1))
            parts.append(cr[at((1, dc)), frame])
            return roll(jnp.concatenate(parts, axis=0), turn, 1)

        mine, right, left = column(0), column(1), column(-1)
        bands = []
        for b in range(BANDS):
            mix = jnp.where(clane // CT == (b + 1) % 4, right, jnp.where(clane // CT == (b + 3) % 4, left, mine))
            bands.append(roll(mix, -CT * b, 1) * mask)
        means.append(bands)
    grad_r = [0.5 * next_minus_prev(x, 0) for x in means[1]]
    grad_c = [0.5 * next_minus_prev(x, 1) for x in means[1]]
    off = [means[1][b] - means[0][b] for b in range(BANDS)]
    now = [jnp.zeros((CROWS, 128), F32)] * 2
    bar = now
    dual_r, dual_c = list(now), list(now)
    data = [jnp.zeros((CROWS, 128), F32)] * BANDS
    for it in range(3):
        div = [0.0, 0.0]
        if it > 0:
            for c in range(2):
                pr = dual_r[c] + (0.5 * SIGMA) * next_minus_prev(bar[c], 0)
                pc = dual_c[c] + (0.5 * SIGMA) * next_minus_prev(bar[c], 1)
                k = shrink(pr * pr + pc * pc) * mask
                dual_r[c], dual_c[c] = pr * k, pc * k
                div[c] = 0.5 * (next_minus_prev(dual_r[c], 0) + next_minus_prev(dual_c[c], 1))
        pull = [0.0, 0.0]
        for b in range(BANDS):
            rho = off[b]
            if it > 0:
                rho = rho + grad_r[b] * bar[0] + grad_c[b] * bar[1]
            data[b] = jnp.clip(data[b] + SIGMA * rho, -LAM, LAM)
            pull = [pull[0] + data[b] * grad_r[b], pull[1] + data[b] * grad_c[b]]
        later = [(now[c] + TAU * (div[c] - pull[c])) * mask for c in range(2)]
        bar = [2.0 * later[c] - now[c] for c in range(2)]
        now = later
    for c in range(2):
        coarse_ref[c] = now[c][8:8 + CT, 0:CT]

    wide_shape = (128, 128 * PANELS)
    wide = lax.broadcasted_iota(jnp.int32, wide_shape, 1)
    source = jnp.where(wide < T + 64, wide // FACTOR, 128 - (128 * PANELS - wide + FACTOR - 1) // FACTOR)
    spread = jnp.where(lax.broadcasted_iota(jnp.int32, wide_shape, 0) == source, 1.0, 0.0).astype(BF16)
    block_lane = lax.broadcasted_iota(jnp.int32, (PANELS, CROWS, 128), 2)
    block_lane = block_lane + 128 * lax.broadcasted_iota(jnp.int32, (PANELS, CROWS, 128), 0)
    block_row = lax.broadcasted_iota(jnp.int32, (PANELS, CROWS, 128), 1) - 8 + me_r * CT
    block_col = jnp.where(block_lane < T + 64, block_lane, block_lane - 128 * PANELS) + me_c * T
    block_mask = jnp.where(
        (block_row >= 0) & (block_row < n_r * CT) & (block_col >= 0) & (block_col < n_c * T), 1.0, 0.0
    )
    for c in range(2):
        repeated = dot_split(now[c], spread, 3)
        t = jnp.stack([repeated[:, 128 * k:128 * k + 128] for k in range(PANELS)])
        first_r = t - roll(t, 1, 1)
        last_r = roll(t, -1, 1) - t
        step_c = across(t)
        square = step_c * step_c
        k_first = shrink(first_r * first_r + square) * block_mask
        k_inner = shrink(square) * block_mask
        k_last = shrink(last_r * last_r + square) * block_mask
        pr_first, pr_last = first_r * k_first, last_r * k_last
        pc_first, pc_inner, pc_last = step_c * k_first, step_c * k_inner, step_c * k_last
        inner = across(pc_inner)
        for n, value in enumerate((
            t, pr_first, pr_last, pc_first, pc_inner, pc_last,
            across(pc_first) - roll(pr_last, 1, 1), inner - pr_first, inner, inner + pr_last,
            across(pc_last) + roll(pr_first, -1, 1),
        )):
            tc[n, c] = value

    def block_row_of(n, c, s):
        return jnp.broadcast_to(tc[n, c, :, pl.ds(s + 7, 1), :], (PANELS, 8, 128))

    panel_sub = lax.broadcasted_iota(jnp.int32, (PANELS, 8, 128), 1)
    right_in = jnp.where(me_c == n_c - 1, 0.0, 1.0)
    left_in = jnp.where(me_c == 0, 0.0, 1.0)
    col_mask = jnp.where(panel_lane[:1] < 64, right_in, left_in)

    def inside_cols(x):
        return jnp.concatenate([x[:2], x[2:] * col_mask], axis=0)

    def clear_rows(ref):
        @pl.when(me_r == 0)
        def _():
            ref[:, :, FIRST:FIRST + 8, :] = jnp.zeros((2, PANELS, 8, 128), F32)

        @pl.when(me_r == n_r - 1)
        def _():
            ref[:, :, OFF + T:OFF + T + 8, :] = jnp.zeros((2, PANELS, 8, 128), F32)

    def opening(s, carry):
        rows = aligned(FIRST + 8 * s)
        for c in range(2):
            t, pr_first, pr_last, pc_first, pc_inner, pc_last, d0, d1, dm, d6, d7 = [
                block_row_of(n, c, s) for n in range(11)
            ]
            at0, at7 = panel_sub == 0, panel_sub == 7
            div = jnp.where(at0, d0, jnp.where(at7, d7, jnp.where(panel_sub == 1, d1, jnp.where(panel_sub == 6, d6, dm))))
            prv[c, :, rows, :] = jnp.where(at0, pr_first, jnp.where(at7, pr_last, 0.0))
            pcv[c, :, rows, :] = jnp.where(at0, pc_first, jnp.where(at7, pc_last, pc_inner))
            later = t + (1.0 / 64.0) * (div - p1[c, :, rows, :])
            u[c, :, rows, :] = later
            ub[c, :, rows, :] = inside_cols(2.0 * later - t)
        return carry

    lax.fori_loop(0, STRIPS, opening, 0, unroll=UNROLL)
    clear_rows(ub)

    for it in (1, 2):
        def dual(s, carry):
            base = FIRST + 8 * s
            rows = aligned(base)
            for c in range(2):
                pr = prv[c, :, rows, :] + (ub[c, :, pl.ds(base + 1, 8), :] - ub[c, :, pl.ds(base - 1, 8), :])
                pc = pcv[c, :, rows, :] + across(ub[c, :, rows, :])
                k = inside_cols(shrink(pr * pr + pc * pc))
                prv[c, :, rows, :] = pr * k
                pcv[c, :, rows, :] = pc * k
            return carry

        lax.fori_loop(0, STRIPS, dual, 0, unroll=UNROLL)
        clear_rows(prv)

        def primal(s, carry):
            base = FIRST + 8 * s
            rows = aligned(base)
            n = PANELS if it < 2 else 2
            step = [(ub[c, :, rows, :] - block_row_of(0, c, s))[:n] for c in range(2)]
            pull = [0.0, 0.0]
            for b in range(BANDS):
                gr, gc = g[b, 0:n, rows, :], g[BANDS + b, 0:n, rows, :]
                value = a[b, 0:n, rows, :] + gr * step[0] + gc * step[1]
                if it == 2:
                    value = value + g[2 * BANDS + b, 0:n, rows, :]
                value = jnp.clip(value, -LAM, LAM)
                if it < 2:
                    a[b, :, rows, :] = value
                pull = [pull[0] + value * gr, pull[1] + value * gc]
            for c in range(2):
                div = (
                    prv[c, 0:n, pl.ds(base + 1, 8), :] - prv[c, 0:n, pl.ds(base - 1, 8), :]
                    + across(pcv[c, :, rows, :])[:n]
                )
                was = u[c, 0:n, rows, :]
                later = was + (1.0 / 64.0) * (div - pull[c])
                if it < 2:
                    u[c, :, rows, :] = later
                    ub[c, :, rows, :] = inside_cols(2.0 * later - was)
                else:
                    for k in range(2):
                        flow_ref[c, aligned(base - OFF), 128 * k:128 * k + 128] = 8.0 * later[k]
            return carry

        if it < 2:
            lax.fori_loop(0, STRIPS, primal, 0, unroll=UNROLL)
            clear_rows(ub)
        else:
            lax.fori_loop(1, STRIPS - 1, primal, 0, unroll=32)


def local(frame_first, frame_second, shifts):
    vmem = pltpu.VMEM
    field = vmem((2, PANELS, ROWS, 128), F32)
    return pl.pallas_call(
        kernel,
        out_shape=(
            vmem((2, T, T), F32),
            vmem((2, CT, CT), F32),
        ),
        in_specs=[
            pl.BlockSpec(memory_space=pl.ANY),
            pl.BlockSpec(memory_space=pl.ANY),
            pl.BlockSpec(memory_space=pltpu.SMEM),
        ],
        out_specs=(pl.BlockSpec(memory_space=vmem), pl.BlockSpec(memory_space=vmem)),
        scratch_shapes=[
            vmem((BANDS, PANELS, ROWS, 128), F32),
            vmem((BANDS, PANELS, ROWS, 128), F32),
            vmem((BANDS, 2, ROWS, 128), F32),
            vmem((3 * BANDS, PANELS, ROWS, 128), F32),
            vmem((BANDS, PANELS, ROWS, 128), F32),
            field, field, field, field, field,
            vmem((11, 2, PANELS, CROWS, 128), F32),
            vmem((2, CROWS, 128), F32),
            vmem((2, 2, 8, 128), F32),
            vmem((8, 2, 8, 128), F32),
            vmem((T, 128), F32),
            vmem((2, T // 2, 128), F32),
            vmem((2, T // 2, 128), F32),
            vmem((8, 16, 128), F32),
            vmem((ROWS, 128), F32),
            vmem((ROWS, 128), F32),
            vmem((8, 128), jnp.int32),
            vmem((8, 8, 128), jnp.int32),
            pltpu.SemaphoreType.DMA((4,)),
            pltpu.SemaphoreType.DMA((32,)),
            pltpu.SemaphoreType.DMA((32,)),
        ],
        compiler_params=pltpu.CompilerParams(
            collective_id=0, has_side_effects=True, vmem_limit_bytes=60 * 1024 * 1024
        ),
    )(frame_first, frame_second, shifts)


def solution(mesh):
    return jax.shard_map(
        local,
        mesh=mesh,
        in_specs=(P(None, "row", "col"), P(None, "row", "col"), P("row", "col", None)),
        out_specs=(P(None, "row", "col"), P(None, "row", "col")),
        check_vma=False,
    )
```
